256 devices in a mesh: freq: 4 (over x_hi, core), strip: 64 (over z, y, x_lo).
Axes of the slice: x: 4 (x_hi: 2, x_lo: 2; x = x_hi * 2 + x_lo), y: 4, z: 8, core: 2. Of those that a mesh axis runs over, the one named last changes fastest.
Arguments:
- source_field: bfloat16 [2, 4, 2, 2048, 2048], P(None, 'freq', None, 'strip'), may hold values from -6 to 6
- recorded: bfloat16 [2, 4, 2, 2048, 2048], P(None, 'freq', None, 'strip'), may hold values from -6 to 6
- phase_index: int32 [1, 2, 4], replicated, may hold values from 0 to 7
- slowness: float32 [16, 2048, 2048], P(None, 'strip'), may hold values from 0.8 to 1.2
- slice_index: int32 [4], replicated, may hold values from 0 to 15
Outputs:
- images: float32 [4, 2048, 2048], P(None, 'strip', 'freq')
The draws below stay inside these ranges and needn't reach their ends.
All inputs are finite; a program needn't handle non-finite values.
Results may differ from the reference program's by a relative error of at most 0.0003.
Values sent between devices are 32-bit elements; how exact they have to be, the bound alone decides.
No kernel may reach another device: no remote copies, remote signals or barrier semaphores. Data moves between devices by JAX's collectives and lax.ppermute only.
A program may use at most 128 MiB of HBM per device.

```python
import math
import jax
import jax.numpy as jnp
from jax import lax

NX = 2048
NY = 2048
SUPER = 1
COMP = 2
FREQS = 4
DEPTHS = 4
SLICES = 16
PHASES = 8


def plant(values, rng, low, top_value):
    place = [jax.random.randint(jax.random.fold_in(rng, axis), (), 0, length) for axis, length in enumerate(values.shape)]
    longest = values.shape.index(max(values.shape))
    beside = place[:longest] + [(place[longest] + 1) % values.shape[longest]] + place[longest + 1:]
    return values.at[tuple(place)].set(low).at[tuple(beside)].set(top_value)


def levels(rng, dims, shards, low, top_value):
    loudness = 1.0
    for dim, parts in shards:
        steps = jax.random.uniform(jax.random.fold_in(jax.random.fold_in(rng, 6), dim), (parts,), jnp.float32, low / len(shards), top_value / len(shards))
        loudness = loudness * jnp.repeat(jnp.exp(steps), dims[dim] // parts).reshape((-1,) + (1,) * (len(dims) - 1 - dim))
    return loudness


def scatter_about(rng, extent, deviation, bound, shards=(), held_as=jnp.bfloat16):
    drawn = deviation * jax.random.normal(rng, extent, jnp.float32)
    if shards:
        drawn = drawn * levels(rng, extent, shards, -0.22, 0.18)
    return jnp.clip(drawn, -bound, bound).astype(held_as)


def setup_inputs(seed: int = 0) -> dict:
    key_of = jax.random.split(jax.random.key(seed), 6)
    return {
        "source_field": scatter_about(key_of[0], (COMP, FREQS, 2, NX, NY), 1.0, 6.0, ((1, 4), (3, 64))),
        "recorded": scatter_about(key_of[1], (COMP, FREQS, 2, NX, NY), 1.0, 6.0, ((1, 4), (3, 64))),
        "phase_index": plant(jax.random.randint(key_of[2], (SUPER, COMP, FREQS), 0, PHASES), jax.random.fold_in(key_of[2], 1), 0, PHASES - 1).astype(jnp.int32),
        "slowness": jnp.clip(0.8 + 0.40000004 * jax.random.uniform(key_of[3], (SLICES, NX, NY), jnp.float32) ** levels(key_of[3], (SLICES, NX, NY), ((1, 64),), -0.2, 0.2), 0.8, 1.2),
        "slice_index": plant(jax.random.randint(key_of[4], (DEPTHS,), 0, SLICES), jax.random.fold_in(key_of[4], 1), 0, SLICES - 1).astype(jnp.int32),
    }


grid_step = 4.0
depth_step = 8.0

def wavenumbers(total_count):
    position = jnp.arange(total_count, dtype=jnp.int32)
    signed = jnp.where(position < total_count // 2, position, position - total_count).astype(jnp.float32)
    return signed * (2.0 * math.pi / (total_count * grid_step))

def frequencies(first_index, local_count, total_count):
    position = (first_index + jnp.arange(local_count, dtype=jnp.int32)).astype(jnp.float32)
    return 0.5 + 1.5 * (position + 0.5) / total_count

def propagator(angular, wave_x, wave_y):
    vertical_sq = angular * angular - wave_x * wave_x - wave_y * wave_y
    vertical = jnp.sqrt(jnp.abs(vertical_sq))
    propagating = vertical_sq > 0
    real_part = jnp.where(propagating, jnp.cos(depth_step * vertical), jnp.exp(-depth_step * vertical))
    imag_part = jnp.where(propagating, jnp.sin(depth_step * vertical), 0.0)
    return (real_part, imag_part)

def encode(wavefield, encode_angle):
    turn_cos = jnp.cos(encode_angle)[:, :, :, None, None]
    turn_sin = jnp.sin(encode_angle)[:, :, :, None, None]
    real_part = wavefield[:, :, 0].astype(jnp.float32)[None]
    imag_part = wavefield[:, :, 1].astype(jnp.float32)[None]
    return (lax.optimization_barrier(jnp.sum(turn_cos * real_part - turn_sin * imag_part, axis=1)), lax.optimization_barrier(jnp.sum(turn_cos * imag_part + turn_sin * real_part, axis=1)))

def reference(source_field, recorded, phase_index, slowness, slice_index):
    encode_angle = phase_index.astype(jnp.float32) * (2.0 * math.pi / PHASES)
    source_real, source_imag = encode(source_field, encode_angle)
    receiver_real, receiver_imag = encode(recorded, encode_angle)
    source = lax.complex(source_real, source_imag)
    receiver = lax.complex(receiver_real, receiver_imag)
    angular = frequencies(0, FREQS, FREQS)
    forward_real, forward_imag = propagator(angular[:, None, None], wavenumbers(NX)[None, :, None], wavenumbers(NY)[None, None, :])
    forward = lax.complex(forward_real, forward_imag)
    backward = lax.complex(forward_real, -forward_imag)
    pictures = []
    for descent in range(DEPTHS):
        slow_slice = lax.dynamic_index_in_dim(slowness, slice_index[descent], 0, keepdims=False)
        rotation = depth_step * angular[:, None, None] * (slow_slice[None] - 1.0)
        source = jnp.fft.ifft2(jnp.fft.fft2(source) * forward) * lax.complex(jnp.cos(rotation), jnp.sin(rotation))
        receiver = jnp.fft.ifft2(jnp.fft.fft2(receiver) * backward) * lax.complex(jnp.cos(rotation), -jnp.sin(rotation))
        product = jnp.real(source) * jnp.real(receiver) + jnp.imag(source) * jnp.imag(receiver)
        pictures.append(lax.optimization_barrier(jnp.sum(product, axis=(0, 1))) / FREQS)
    return jnp.stack(pictures)
```

```python
import functools
import math

import jax
import jax.numpy as jnp
import numpy as np
from jax import lax
from jax.experimental import pallas as pl
from jax.experimental.pallas import tpu as pltpu
from jax.sharding import PartitionSpec as P

DEPTHS = 4
PHASES = 8
SIZE = 2048
RADIX = 16
INNER = SIZE // RADIX
HALF = 64
ROWS = 64
VMEM_LIMIT = 40 * 1024 * 1024

grid_step = 4.0
depth_step = 8.0


def split_table(table):
    high = table.astype(jnp.bfloat16)
    low = (table - high.astype(np.float64)).astype(jnp.bfloat16)
    return high, low


def inner_dft(direction):
    index = np.arange(INNER)
    angle = direction * 2.0 * np.pi * (np.outer(index, index) % INNER) / INNER
    return np.cos(angle), np.sin(angle)


def lane_tables():
    cosine, sine = inner_dft(-1.0)
    real_columns = np.concatenate([cosine, -sine], axis=0)
    imag_columns = np.concatenate([sine, cosine], axis=0)
    forward = np.concatenate(
        [
            part[:, half * HALF : (half + 1) * HALF]
            for half in range(2)
            for part in (real_columns, imag_columns)
        ],
        axis=1,
    )
    cosine, sine = inner_dft(1.0)
    real_rows = np.concatenate([cosine, sine], axis=1)
    imag_rows = np.concatenate([-sine, cosine], axis=1)
    inverse = (
        np.concatenate(
            [
                part[half * HALF : (half + 1) * HALF]
                for half in range(2)
                for part in (real_rows, imag_rows)
            ],
            axis=0,
        )
        / SIZE
    )
    out = []
    for table in (forward, inverse):
        high, low = split_table(table)
        out.append(np.concatenate([high, low, high], axis=0))
    return out


def row_tables():
    out = []
    for direction, scale in ((-1.0, 1.0), (1.0, 1.0 / SIZE)):
        cosine, sine = inner_dft(direction)
        high, low = split_table(np.concatenate([cosine, sine], axis=0) * scale)
        out.append(np.concatenate([high, low, high], axis=1))
    return out


def twiddles():
    angle = -2.0 * np.pi * np.outer(np.arange(RADIX), np.arange(INNER)) / SIZE
    return np.cos(angle), np.sin(angle)


def lane_twiddles():
    cosine, sine = twiddles()
    return np.concatenate([cosine, sine], axis=1).astype(np.float32)


def row_twiddles():
    cosine, sine = twiddles()
    sign = np.where(np.arange(2 * HALF) < HALF, -1.0, 1.0)
    return (
        np.broadcast_to(cosine[:, :, None], (RADIX, INNER, 2 * HALF)).astype(np.float32),
        (sine[:, :, None] * sign[None, None, :]).astype(np.float32),
    )


def butterfly16(values, direction, add, sub, turn, scale_by):
    def four(a, b, c, d):
        even_sum, even_diff = add(a, c), sub(a, c)
        odd_sum, odd_diff = add(b, d), turn(sub(b, d), direction)
        return [
            add(even_sum, odd_sum),
            add(even_diff, odd_diff),
            sub(even_sum, odd_sum),
            sub(even_diff, odd_diff),
        ]

    first = [four(*[values[4 * n + m] for n in range(4)]) for m in range(4)]
    result = [None] * 16
    for k in range(4):
        column = []
        for m in range(4):
            value = first[m][k]
            power = m * k
            if power == 4:
                value = turn(value, direction)
            elif power:
                angle = direction * 2.0 * math.pi * power / 16
                value = scale_by(value, math.cos(angle), math.sin(angle))
            column.append(value)
        for m, value in enumerate(four(*column)):
            result[k + 4 * m] = value
    return result


def pair_add(a, b):
    return (a[0] + b[0], a[1] + b[1])


def pair_sub(a, b):
    return (a[0] - b[0], a[1] - b[1])


def pair_turn(a, s):
    return (-a[1], a[0]) if s > 0 else (a[1], -a[0])


def pair_scale(a, c, s):
    return (a[0] * c - a[1] * s, a[0] * s + a[1] * c)


def swap_halves(value):
    return pltpu.roll(value, HALF, 1)


def half_sign():
    lane = lax.broadcasted_iota(jnp.int32, (8, 2 * HALF), 1)
    return jnp.where(lane < HALF, -1.0, 1.0).astype(jnp.float32)


def split_value(value):
    high = value.astype(jnp.bfloat16)
    low = (value - high.astype(jnp.float32)).astype(jnp.bfloat16)
    return high, low


def sine_cosine(angle):
    turns = jnp.round(angle * (2.0 / math.pi))
    rest = angle - turns * 1.5703125
    rest = rest - turns * 4.8375129699707031e-4
    rest = rest - turns * 7.5497899548918821e-8
    square = rest * rest
    sine = rest + rest * square * (
        -1.6666654611e-1 + square * (8.3321608736e-3 - square * 1.9515295891e-4)
    )
    cosine = (
        1.0
        - 0.5 * square
        + square
        * square
        * (4.166664568298827e-2 + square * (-1.388731625493765e-3 + square * 2.443315711809948e-5))
    )
    quarter = turns.astype(jnp.int32)
    odd = (quarter & 1) == 1
    sine_out = jnp.where(odd, cosine, sine)
    cosine_out = jnp.where(odd, sine, cosine)
    sine_out = jnp.where((quarter & 2) == 2, -sine_out, sine_out)
    cosine_out = jnp.where(((quarter + 1) & 2) == 2, -cosine_out, cosine_out)
    return sine_out, cosine_out


def lanes(a):
    return slice(a * INNER, (a + 1) * INNER)


def forward_rows(wave, work, table, twiddle, out):
    @pl.loop(0, ROWS // 8)
    def _(tile):
        rows = pl.ds(tile * 8, 8)
        values = [(wave[0, rows, lanes(a)], wave[1, rows, lanes(a)]) for a in range(RADIX)]
        values = butterfly16(values, -1.0, pair_add, pair_sub, pair_turn, pair_scale)
        for k, (real, imag) in enumerate(values):
            if k:
                cosine = twiddle[k : k + 1, :INNER]
                sine = twiddle[k : k + 1, INNER:]
                real, imag = real * cosine - imag * sine, real * sine + imag * cosine
            work[k, rows, :INNER] = real
            work[k, rows, INNER:] = imag

    for group in range(0, RADIX, 4):
        value = work[group : group + 4].reshape(4 * ROWS, 2 * INNER)
        high, low = split_value(value)
        result = jnp.dot(
            jnp.concatenate([high, high, low], axis=1),
            table[...],
            preferred_element_type=jnp.float32,
        )
        result = result.reshape(4, ROWS, 2 * INNER)
        for k in range(4):
            for kind in range(2):
                for half in range(2):
                    out[(kind * RADIX + group + k) * 2 + half] = result[
                        k,
                        kind * (ROWS // 2) : (kind + 1) * (ROWS // 2),
                        half * INNER : (half + 1) * INNER,
                    ]


def inverse_rows(chunks, work, table, twiddle, wave):
    for group in range(0, RADIX, 4):
        parts = []
        for k in range(4):
            for kind in range(2):
                place = (kind * RADIX + group + k) * 2
                parts.append(jnp.concatenate([chunks[place], chunks[place + 1]], axis=1))
        high, low = split_value(jnp.concatenate(parts, axis=0))
        result = jnp.dot(
            jnp.concatenate([high, high, low], axis=1),
            table[...],
            preferred_element_type=jnp.float32,
        )
        work[group : group + 4] = result.reshape(4, ROWS, 2 * INNER)

    @pl.loop(0, ROWS // 8)
    def _(tile):
        rows = pl.ds(tile * 8, 8)
        values = []
        for k in range(RADIX):
            real, imag = work[k, rows, :INNER], work[k, rows, INNER:]
            if k:
                cosine = twiddle[k : k + 1, :INNER]
                sine = twiddle[k : k + 1, INNER:]
                real, imag = real * cosine + imag * sine, imag * cosine - real * sine
            values.append((real, imag))
        values = butterfly16(values, 1.0, pair_add, pair_sub, pair_turn, pair_scale)
        for a, (real, imag) in enumerate(values):
            wave[0, rows, lanes(a)] = real
            wave[1, rows, lanes(a)] = imag


def rotate_and_image(wave, slow, angular, image, keep):
    half_rows = ROWS // 2
    parts = image.shape[0]
    width = SIZE // parts

    @pl.loop(0, half_rows // 8)
    def _(tile):
        first = pl.ds(tile * 8, 8)
        second = pl.ds(half_rows + tile * 8, 8)
        for a in range(SIZE // 512):
            columns = slice(a * 512, (a + 1) * 512)
            sine, cosine = sine_cosine(angular * (slow[0, first, columns] - 1.0))
            turned = []
            for rows in (first, second):
                real, imag = wave[0, rows, columns], wave[1, rows, columns]
                real, imag = real * cosine - imag * sine, real * sine + imag * cosine
                if keep:
                    wave[0, rows, columns] = real
                    wave[1, rows, columns] = imag
                turned.append((real, imag))
            picture = turned[0][0] * turned[1][0] - turned[0][1] * turned[1][1]
            place = a * 512 // width
            offset = a * 512 % width
            image[place, first, offset : offset + 512] = picture * 0.25


def first_kernel(turn_ref, source, recorded, table, twiddle, out, wave, work):
    half_rows = ROWS // 2

    @pl.loop(0, half_rows // 16)
    def _(tile):
        rows = pl.ds(tile * 16, 16)
        for kind, field in enumerate((source, recorded)):
            place = pl.ds(kind * half_rows + tile * 16, 16)
            for a in range(SIZE // 512):
                columns = slice(a * 512, (a + 1) * 512)
                real_sum, imag_sum = None, None
                for shot in range(field.shape[0]):
                    real = field[shot, 0, 0, rows, columns].astype(jnp.float32)
                    imag = field[shot, 0, 1, rows, columns].astype(jnp.float32)
                    cosine, sine = turn_ref[0, shot], turn_ref[1, shot]
                    real_part = cosine * real - sine * imag
                    imag_part = cosine * imag + sine * real
                    real_sum = real_part if real_sum is None else real_sum + real_part
                    imag_sum = imag_part if imag_sum is None else imag_sum + imag_part
                wave[0, place, columns] = real_sum
                wave[1, place, columns] = imag_sum if kind == 0 else -imag_sum

    forward_rows(wave, work, table, twiddle, out)


def middle_kernel(
    index_ref, angular_ref, chunks, slow, inverse_table, table, twiddle, out, image, wave, work
):
    inverse_rows(chunks, work, inverse_table, twiddle, wave)
    rotate_and_image(wave, slow, angular_ref[0], image, True)
    forward_rows(wave, work, table, twiddle, out)


def last_kernel(index_ref, angular_ref, chunks, slow, inverse_table, twiddle, image, wave, work):
    inverse_rows(chunks, work, inverse_table, twiddle, wave)
    rotate_and_image(wave, slow, angular_ref[0], image, False)


WAVE = pltpu.VMEM((2, ROWS, SIZE), jnp.float32)
WORK = pltpu.VMEM((RADIX, ROWS, 2 * INNER), jnp.float32)
CHUNKS = jax.ShapeDtypeStruct((64, ROWS // 2, 2 * HALF), jnp.float32)


def whole():
    return pl.BlockSpec(memory_space=pltpu.VMEM)


def params():
    return pltpu.CompilerParams(vmem_limit_bytes=VMEM_LIMIT)


def first_step(turn, source, recorded, table, twiddle):
    return pl.pallas_call(
        first_kernel,
        out_shape=CHUNKS,
        in_specs=[pl.BlockSpec(memory_space=pltpu.SMEM)] + [whole()] * 4,
        out_specs=whole(),
        scratch_shapes=[WAVE, WORK],
        compiler_params=params(),
        name="encode_forward",
    )(turn, source, recorded, table, twiddle)


def space_step(slice_at, angular, chunks, slowness, tables, twiddle, parts, last):
    rows = ROWS // 2

    def fixed(shape):
        return pl.BlockSpec(shape, lambda i, *scalars: (0,) * len(shape))

    image = jax.ShapeDtypeStruct((parts, rows, SIZE // parts), jnp.float32)
    constants = [tables[1], twiddle] if last else [tables[1], tables[0], twiddle]
    out_shape = [image] if last else [CHUNKS, image]
    return pl.pallas_call(
        last_kernel if last else middle_kernel,
        out_shape=out_shape,
        grid_spec=pltpu.PrefetchScalarGridSpec(
            num_scalar_prefetch=2,
            grid=(1,),
            in_specs=[
                fixed(chunks.shape),
                pl.BlockSpec((1, rows, SIZE), lambda i, place, angle: (place[0], 0, 0)),
            ]
            + [fixed(c.shape) for c in constants],
            out_specs=[fixed(o.shape) for o in out_shape],
            scratch_shapes=[WAVE, WORK],
        ),
        compiler_params=params(),
        name="space_last" if last else "space_step",
    )(slice_at, angular, chunks, slowness, *constants)


def spectral_kernel(chunks, left, left_inverse, twiddle_cos, twiddle_sin, prop_a, prop_b, out, work):
    sign = half_sign()

    def turn(value, direction):
        return swap_halves(value) * (sign if direction > 0 else -sign)

    def scale_by(value, c, s):
        return value * c + swap_halves(value) * (sign * s)

    def add(a, b):
        return a + b

    def sub(a, b):
        return a - b

    tile_rows = 8
    per_chunk = chunks.shape[1]

    def place(a, tile):
        row = a * INNER + tile * tile_rows
        return row // per_chunk, row % per_chunk

    for tile in range(INNER // tile_rows):
        rows = slice(tile * tile_rows, (tile + 1) * tile_rows)
        values = []
        for a in range(RADIX):
            chunk, row = place(a, tile)
            values.append(chunks[chunk, row : row + tile_rows, :])
        values = butterfly16(values, -1.0, add, sub, turn, scale_by)
        for k, value in enumerate(values):
            if k:
                value = value * twiddle_cos[k, rows] + swap_halves(value) * twiddle_sin[k, rows]
            work[k, rows] = value

    wide_sign = jnp.concatenate([sign, sign], axis=1)[:1]

    def multiply(matrix, value):
        high, low = split_value(value)
        result = jnp.dot(
            matrix[...],
            jnp.concatenate([high, high, low], axis=0),
            preferred_element_type=jnp.float32,
        )
        swapped = jnp.concatenate(
            [swap_halves(result[INNER:, :INNER]), swap_halves(result[INNER:, INNER:])], axis=1
        )
        return result[:INNER] + swapped * wide_sign

    for pair in range(0, RADIX, 2):
        value = jnp.concatenate([work[pair], work[pair + 1]], axis=1)
        value = multiply(left, value)
        shifted = []
        for k in range(2):
            part = value[:, k * INNER : (k + 1) * INNER]
            shifted.append(part * prop_a[pair + k] + swap_halves(part) * prop_b[pair + k])
        value = multiply(left_inverse, jnp.concatenate(shifted, axis=1))
        work[pair] = value[:, :INNER]
        work[pair + 1] = value[:, INNER:]

    for tile in range(INNER // tile_rows):
        rows = slice(tile * tile_rows, (tile + 1) * tile_rows)
        values = []
        for k in range(RADIX):
            value = work[k, rows]
            if k:
                value = value * twiddle_cos[k, rows] - swap_halves(value) * twiddle_sin[k, rows]
            values.append(value)
        values = butterfly16(values, 1.0, add, sub, turn, scale_by)
        for a, value in enumerate(values):
            chunk, row = place(a, tile)
            out[chunk, row : row + tile_rows, :] = value


def spectral_step(chunks, left_tables, row_twiddle, propagators):
    return pl.pallas_call(
        spectral_kernel,
        out_shape=jax.ShapeDtypeStruct(chunks.shape, jnp.float32),
        in_specs=[whole()] * 7,
        out_specs=whole(),
        scratch_shapes=[pltpu.VMEM((RADIX, INNER, 2 * HALF), jnp.float32)],
        compiler_params=params(),
        name="spectral_step",
    )(chunks, *left_tables, *row_twiddle, *propagators)


def wavenumber(index):
    signed = jnp.where(index < SIZE // 2, index, index - SIZE).astype(jnp.float32)
    return signed * (2.0 * math.pi / (SIZE * grid_step))


def propagator_tables(angular, strip):
    block = strip % (2 * RADIX)
    lane = jnp.arange(2 * HALF, dtype=jnp.int32) % HALF
    column = block // 2 + RADIX * ((block % 2) * HALF + lane)
    wave_y = wavenumber(column)[None, None, :]
    row = (
        jnp.arange(RADIX, dtype=jnp.int32)[:, None]
        + RADIX * jnp.arange(INNER, dtype=jnp.int32)[None, :]
    )
    wave_x = wavenumber(row)[:, :, None]
    vertical_sq = angular * angular - wave_x * wave_x - wave_y * wave_y
    vertical = jnp.sqrt(jnp.abs(vertical_sq))
    propagating = vertical_sq > 0
    sine, cosine = sine_cosine(depth_step * vertical)
    real_part = jnp.where(propagating, cosine, jnp.exp(-depth_step * vertical))
    imag_part = jnp.where(propagating, sine, 0.0)
    sign = jnp.where(jnp.arange(2 * HALF) < HALF, -1.0, 1.0).astype(jnp.float32)
    return real_part, imag_part * sign[None, None, :]


def per_device(source_field, recorded, phase_index, slowness, slice_index):
    freq = lax.axis_index("freq")
    strip = lax.axis_index("strip")
    parts = lax.axis_size("freq")
    total_freq = source_field.shape[1] * parts
    encode_angle = lax.dynamic_slice_in_dim(phase_index, freq, 1, 2)[0, :, 0].astype(
        jnp.float32
    ) * (2.0 * math.pi / PHASES)
    turn = jnp.stack([jnp.cos(encode_angle), jnp.sin(encode_angle)])
    angular = 0.5 + 1.5 * (freq.astype(jnp.float32) + 0.5) / total_freq

    right = [jnp.asarray(t) for t in lane_tables()]
    left = [jnp.asarray(t) for t in row_tables()]
    lane_twiddle = jnp.asarray(lane_twiddles())
    row_twiddle = [jnp.asarray(t) for t in row_twiddles()]
    propagators = propagator_tables(angular, strip)

    def exchange(chunks):
        return lax.all_to_all(chunks, "strip", 0, 0, tiled=True)

    chunks = first_step(turn, source_field, recorded, right[0], lane_twiddle)
    scaled = (depth_step * angular)[None]
    pictures = []
    for descent in range(DEPTHS):
        chunks = exchange(chunks)
        chunks = spectral_step(chunks, left, row_twiddle, propagators)
        chunks = exchange(chunks)
        last = descent == DEPTHS - 1
        result = space_step(
            slice_index[descent : descent + 1],
            scaled,
            chunks,
            slowness,
            right,
            lane_twiddle,
            parts,
            last,
        )
        if last:
            image = result[0]
            pictures.append(jnp.sum(lax.all_to_all(image, "freq", 0, 0, tiled=True), axis=0))
        else:
            chunks, image = result
            pictures.append(lax.psum_scatter(image, "freq", scatter_dimension=0, tiled=False))
    return jnp.stack(pictures)


def solution(mesh):
    placed = (
        P(None, "freq", None, "strip", None),
        P(None, "freq", None, "strip", None),
        P(),
        P(None, "strip", None),
        P(),
    )
    return jax.shard_map(
        per_device, mesh=mesh, in_specs=placed, out_specs=P(None, "strip", "freq"), check_vma=False
    )
```

```python
import functools
import math

import jax
import jax.numpy as jnp
import numpy as np
from jax import lax
from jax.experimental import pallas as pl
from jax.experimental.pallas import tpu as pltpu
from jax.sharding import Mesh
from jax.sharding import PartitionSpec as P

DEPTHS = 4
PHASES = 8
SIZE = 2048
RADIX = 16
INNER = SIZE // RADIX
HALF = 64
ROWS = 64
VMEM_LIMIT = 12 * 1024 * 1024

grid_step = 4.0
depth_step = 8.0


def split_table(table):
    high = table.astype(jnp.bfloat16)
    low = (table - high.astype(np.float64)).astype(jnp.bfloat16)
    return high, low


def inner_dft(direction):
    index = np.arange(INNER)
    angle = direction * 2.0 * np.pi * (np.outer(index, index) % INNER) / INNER
    return np.cos(angle), np.sin(angle)


def lane_tables():
    cosine, sine = inner_dft(-1.0)
    real_columns = np.concatenate([cosine, -sine], axis=0)
    imag_columns = np.concatenate([sine, cosine], axis=0)
    forward = np.concatenate(
        [
            part[:, half * HALF : (half + 1) * HALF]
            for half in range(2)
            for part in (real_columns, imag_columns)
        ],
        axis=1,
    )
    cosine, sine = inner_dft(1.0)
    real_rows = np.concatenate([cosine, sine], axis=1)
    imag_rows = np.concatenate([-sine, cosine], axis=1)
    inverse = (
        np.concatenate(
            [
                part[half * HALF : (half + 1) * HALF]
                for half in range(2)
                for part in (real_rows, imag_rows)
            ],
            axis=0,
        )
        / SIZE
    )
    out = []
    for table in (forward, inverse):
        high, low = split_table(table)
        out.append(np.concatenate([high, low, high], axis=0))
    return out


def row_tables():
    out = []
    for direction, scale in ((-1.0, 1.0), (1.0, 1.0 / SIZE)):
        cosine, sine = inner_dft(direction)
        high, low = split_table(np.concatenate([cosine, sine], axis=0) * scale)
        out.append(np.concatenate([high, low, high], axis=1))
    return out


def twiddles():
    angle = -2.0 * np.pi * np.outer(np.arange(RADIX), np.arange(INNER)) / SIZE
    return np.cos(angle), np.sin(angle)


def lane_twiddles():
    cosine, sine = twiddles()
    return np.concatenate([cosine, sine], axis=1).astype(np.float32)


def row_twiddles():
    cosine, sine = twiddles()
    sign = np.where(np.arange(2 * HALF) < HALF, -1.0, 1.0)
    ones = np.ones(2 * HALF)
    return np.stack(
        [cosine[:, :8, None] * ones, sine[:, :8, None] * sign]
    ).astype(np.float32)


def butterfly16(values, direction, add, sub, turn, scale_by):
    def four(a, b, c, d):
        even_sum, even_diff = add(a, c), sub(a, c)
        odd_sum, odd_diff = add(b, d), turn(sub(b, d), direction)
        return [
            add(even_sum, odd_sum),
            add(even_diff, odd_diff),
            sub(even_sum, odd_sum),
            sub(even_diff, odd_diff),
        ]

    first = [four(*[values[4 * n + m] for n in range(4)]) for m in range(4)]
    result = [None] * 16
    for k in range(4):
        column = []
        for m in range(4):
            value = first[m][k]
            power = m * k
            if power == 4:
                value = turn(value, direction)
            elif power:
                angle = direction * 2.0 * math.pi * power / 16
                value = scale_by(value, math.cos(angle), math.sin(angle))
            column.append(value)
        for m, value in enumerate(four(*column)):
            result[k + 4 * m] = value
    return result


def pair_add(a, b):
    return (a[0] + b[0], a[1] + b[1])


def pair_sub(a, b):
    return (a[0] - b[0], a[1] - b[1])


def pair_turn(a, s):
    return (-a[1], a[0]) if s > 0 else (a[1], -a[0])


def pair_scale(a, c, s):
    return (a[0] * c - a[1] * s, a[0] * s + a[1] * c)


def swap_halves(value):
    return pltpu.roll(value, HALF, 1)


def half_sign():
    lane = lax.broadcasted_iota(jnp.int32, (8, 2 * HALF), 1)
    return jnp.where(lane < HALF, -1.0, 1.0).astype(jnp.float32)


def split_value(value):
    high = value.astype(jnp.bfloat16)
    low = (value - high.astype(jnp.float32)).astype(jnp.bfloat16)
    return high, low


def sine_cosine(angle):
    turns = jnp.round(angle * (2.0 / math.pi))
    rest = angle - turns * 1.5703125
    rest = rest - turns * 4.8375129699707031e-4
    rest = rest - turns * 7.5497899548918821e-8
    square = rest * rest
    sine = rest + rest * square * (
        -1.6666654611e-1 + square * (8.3321608736e-3 - square * 1.9515295891e-4)
    )
    cosine = (
        1.0
        - 0.5 * square
        + square
        * square
        * (4.166664568298827e-2 + square * (-1.388731625493765e-3 + square * 2.443315711809948e-5))
    )
    quarter = turns.astype(jnp.int32)
    odd = (quarter & 1) == 1
    sine_out = jnp.where(odd, cosine, sine)
    cosine_out = jnp.where(odd, sine, cosine)
    sine_out = jnp.where((quarter & 2) == 2, -sine_out, sine_out)
    cosine_out = jnp.where(((quarter + 1) & 2) == 2, -cosine_out, cosine_out)
    return sine_out, cosine_out


def lanes(a):
    return slice(a * INNER, (a + 1) * INNER)


def forward_rows(wave, work, table, twiddle, out):
    @pl.loop(0, ROWS // 8)
    def _(tile):
        rows = pl.ds(tile * 8, 8)
        values = [(wave[0, rows, lanes(a)], wave[1, rows, lanes(a)]) for a in range(RADIX)]
        values = butterfly16(values, -1.0, pair_add, pair_sub, pair_turn, pair_scale)
        for k, (real, imag) in enumerate(values):
            if k:
                cosine = twiddle[k : k + 1, :INNER]
                sine = twiddle[k : k + 1, INNER:]
                real, imag = real * cosine - imag * sine, real * sine + imag * cosine
            work[k, rows, :INNER] = real
            work[k, rows, INNER:] = imag

    for group in range(0, RADIX, 4):
        value = work[group : group + 4].reshape(4 * ROWS, 2 * INNER)
        high, low = split_value(value)
        result = jnp.dot(
            jnp.concatenate([high, high, low], axis=1),
            table[...],
            preferred_element_type=jnp.float32,
        )
        result = result.reshape(4, ROWS, 2 * INNER)
        for k in range(4):
            for kind in range(2):
                for half in range(2):
                    out[(kind * RADIX + group + k) * 2 + half] = result[
                        k,
                        kind * (ROWS // 2) : (kind + 1) * (ROWS // 2),
                        half * INNER : (half + 1) * INNER,
                    ]


def inverse_rows(chunks, work, table, twiddle, wave):
    for group in range(0, RADIX, 4):
        parts = []
        for k in range(4):
            for kind in range(2):
                place = (kind * RADIX + group + k) * 2
                parts.append(jnp.concatenate([chunks[place], chunks[place + 1]], axis=1))
        high, low = split_value(jnp.concatenate(parts, axis=0))
        result = jnp.dot(
            jnp.concatenate([high, high, low], axis=1),
            table[...],
            preferred_element_type=jnp.float32,
        )
        work[group : group + 4] = result.reshape(4, ROWS, 2 * INNER)

    @pl.loop(0, ROWS // 8)
    def _(tile):
        rows = pl.ds(tile * 8, 8)
        values = []
        for k in range(RADIX):
            real, imag = work[k, rows, :INNER], work[k, rows, INNER:]
            if k:
                cosine = twiddle[k : k + 1, :INNER]
                sine = twiddle[k : k + 1, INNER:]
                real, imag = real * cosine + imag * sine, imag * cosine - real * sine
            values.append((real, imag))
        values = butterfly16(values, 1.0, pair_add, pair_sub, pair_turn, pair_scale)
        for a, (real, imag) in enumerate(values):
            wave[0, rows, lanes(a)] = real
            wave[1, rows, lanes(a)] = imag


def rotate_and_image(wave, slow, angular, image, keep):
    half_rows = ROWS // 2
    width = image.shape[3]

    @pl.loop(0, half_rows // 8)
    def _(tile):
        first = pl.ds(tile * 8, 8)
        second = pl.ds(half_rows + tile * 8, 8)
        for a in range(SIZE // 512):
            columns = slice(a * 512, (a + 1) * 512)
            sine, cosine = sine_cosine(angular * (slow[tile, :, columns] - 1.0))
            turned = []
            for rows in (first, second):
                real, imag = wave[0, rows, columns], wave[1, rows, columns]
                real, imag = real * cosine - imag * sine, real * sine + imag * cosine
                if keep:
                    wave[0, rows, columns] = real
                    wave[1, rows, columns] = imag
                turned.append((real, imag))
            picture = turned[0][0] * turned[1][0] - turned[0][1] * turned[1][1]
            place = a * 512 // width
            offset = a * 512 % width
            image[tile, place, :, offset : offset + 512] = picture * (1.0 / image.shape[0])


def fetch(pairs, semaphores):
    copies = [
        pltpu.make_async_copy(source, target, semaphores.at[n])
        for n, (source, target) in enumerate(pairs)
    ]
    for copy in copies:
        copy.start()
    return copies


def first_kernel(
    turn_ref, source, recorded, table, twiddle, early, out, wave, work, fields, tables, semaphores
):
    half_rows = ROWS // 2
    copies = fetch(
        [(source, fields.at[0]), (recorded, fields.at[1]), (table.at[0], tables)], semaphores
    )
    for kind in range(2):
        copies[kind].wait()

        @pl.loop(0, half_rows // 16)
        def _(tile):
            rows = pl.ds(tile * 16, 16)
            place = pl.ds(kind * half_rows + tile * 16, 16)
            for a in range(SIZE // 512):
                columns = slice(a * 512, (a + 1) * 512)
                real_sum, imag_sum = None, None
                for shot in range(fields.shape[1]):
                    real = fields[kind, shot, 0, 0, rows, columns].astype(jnp.float32)
                    imag = fields[kind, shot, 0, 1, rows, columns].astype(jnp.float32)
                    cosine, sine = turn_ref[0, shot], turn_ref[1, shot]
                    real_part = cosine * real - sine * imag
                    imag_part = cosine * imag + sine * real
                    real_sum = real_part if real_sum is None else real_sum + real_part
                    imag_sum = imag_part if imag_sum is None else imag_sum + imag_part
                wave[0, place, columns] = real_sum
                wave[1, place, columns] = imag_sum if kind == 0 else -imag_sum

    copies[2].wait()
    forward_rows(wave, work, tables, twiddle, out)


def space_kernel(
    depth, last, angular, chunks, slow, table, twiddle, early, *refs
):
    if last:
        image, wave, work, tables, slow_here, semaphores = refs
    else:
        out, image, wave, work, tables, slow_here, semaphores = refs
    copies = fetch(
        [(table.at[1], tables.at[1]), (slow.at[:, depth], slow_here)]
        + ([] if last else [(table.at[0], tables.at[0])]),
        semaphores,
    )
    copies[0].wait()
    inverse_rows(chunks, work, tables.at[1], twiddle, wave)
    copies[1].wait()
    rotate_and_image(wave, slow_here, angular[0], image, not last)
    if not last:
        copies[2].wait()
        forward_rows(wave, work, tables.at[0], twiddle, out)


WAVE = pltpu.VMEM((2, ROWS, SIZE), jnp.float32)
WORK = pltpu.VMEM((RADIX, ROWS, 2 * INNER), jnp.float32)
CHUNKS = jax.ShapeDtypeStruct((64, ROWS // 2, 2 * HALF), jnp.float32)


def whole():
    return pl.BlockSpec(memory_space=pltpu.VMEM)


def anywhere():
    return pl.BlockSpec(memory_space=pl.ANY)


def scalars():
    return pl.BlockSpec(memory_space=pltpu.SMEM)


def params():
    return pltpu.CompilerParams(vmem_limit_bytes=VMEM_LIMIT)


def first_step(turn, source, recorded, table, twiddle, early):
    return pl.pallas_call(
        first_kernel,
        out_shape=CHUNKS,
        in_specs=[scalars(), anywhere(), anywhere(), anywhere(), whole(), anywhere()],
        out_specs=whole(),
        scratch_shapes=[
            WAVE,
            WORK,
            pltpu.VMEM((2,) + source.shape, source.dtype),
            pltpu.VMEM(table.shape[1:], table.dtype),
            pltpu.SemaphoreType.DMA((3,)),
        ],
        compiler_params=params(),
        name="encode_forward",
    )(turn, source, recorded, table, twiddle, early)


def space_step(angular, chunks, slow, table, twiddle, early, depth, last):
    parts = slow.shape[0]
    image = jax.ShapeDtypeStruct((parts, parts, ROWS // 2 // parts, SIZE // parts), jnp.float32)
    out_shape = [image] if last else [CHUNKS, image]
    return pl.pallas_call(
        functools.partial(space_kernel, depth, last),
        out_shape=out_shape,
        in_specs=[scalars(), whole(), anywhere(), anywhere(), whole(), anywhere()],
        out_specs=[whole()] * len(out_shape),
        scratch_shapes=[
            WAVE,
            WORK,
            pltpu.VMEM(table.shape, table.dtype),
            pltpu.VMEM((slow.shape[0],) + slow.shape[2:], slow.dtype),
            pltpu.SemaphoreType.DMA((2 if last else 3,)),
        ],
        compiler_params=params(),
        name="space_last" if last else "space_step",
    )(angular, chunks, slow, table, twiddle, early)


def spectral_kernel(
    slab_in, chunks, matrices, twiddle, prop_a, prop_b, early, out, work, left, semaphores
):
    copies = fetch([(matrices.at[0], left.at[0]), (matrices.at[1], left.at[1])], semaphores)
    sign = half_sign()

    def turn(value, direction):
        return swap_halves(value) * (sign if direction > 0 else -sign)

    def scale_by(value, c, s):
        return value * c + swap_halves(value) * (sign * s)

    def add(a, b):
        return a + b

    def sub(a, b):
        return a - b

    tile_rows = 8

    def place(slab, a, tile):
        strip, part = a * (INNER // 32) + tile // 4, tile % 4
        if slab:
            return part * 16 + strip % 16, strip // 16 * 8
        return strip, part * 8

    def turn_rows(value, k, tile, direction):
        angle = -2.0 * math.pi * k * tile * tile_rows / SIZE
        cosine, sine = twiddle[0, k], twiddle[1, k]
        if tile:
            c, s = math.cos(angle), math.sin(angle)
            cosine, sine = cosine * c - sine * (sign * s), sine * c + cosine * (sign * s)
        swapped = swap_halves(value) * sine
        return value * cosine - swapped * direction

    for tile in range(INNER // tile_rows):
        rows = slice(tile * tile_rows, (tile + 1) * tile_rows)
        values = []
        for a in range(RADIX):
            chunk, row = place(slab_in, a, tile)
            values.append(chunks[chunk, row : row + tile_rows, :])
        values = butterfly16(values, -1.0, add, sub, turn, scale_by)
        for k, value in enumerate(values):
            if k:
                value = turn_rows(value, k, tile, -1.0)
            work[k, rows] = value

    for copy in copies:
        copy.wait()
    wide_sign = jnp.concatenate([sign, sign], axis=1)[:1]

    def multiply(matrix, value):
        high, low = split_value(value)
        result = jnp.dot(
            matrix[...],
            jnp.concatenate([high, high, low], axis=0),
            preferred_element_type=jnp.float32,
        )
        swapped = jnp.concatenate(
            [swap_halves(result[INNER:, :INNER]), swap_halves(result[INNER:, INNER:])], axis=1
        )
        return result[:INNER] + swapped * wide_sign

    for pair in range(0, RADIX, 2):
        value = jnp.concatenate([work[pair], work[pair + 1]], axis=1)
        value = multiply(left.at[0], value)
        shifted = []
        for k in range(2):
            part = value[:, k * INNER : (k + 1) * INNER]
            shifted.append(part * prop_a[pair + k] + swap_halves(part) * prop_b[pair + k])
        value = multiply(left.at[1], jnp.concatenate(shifted, axis=1))
        work[pair] = value[:, :INNER]
        work[pair + 1] = value[:, INNER:]

    for tile in range(INNER // tile_rows):
        rows = slice(tile * tile_rows, (tile + 1) * tile_rows)
        values = []
        for k in range(RADIX):
            value = work[k, rows]
            if k:
                value = turn_rows(value, k, tile, 1.0)
            values.append(value)
        values = butterfly16(values, 1.0, add, sub, turn, scale_by)
        for a, value in enumerate(values):
            chunk, row = place(True, a, tile)
            out[chunk, row : row + tile_rows, :] = value


def spectral_step(chunks, matrices, twiddle, propagators, early, slab_in):
    return pl.pallas_call(
        functools.partial(spectral_kernel, slab_in),
        out_shape=CHUNKS,
        in_specs=[whole(), anywhere(), whole(), whole(), whole(), anywhere()],
        out_specs=whole(),
        scratch_shapes=[
            pltpu.VMEM((RADIX, INNER, 2 * HALF), jnp.float32),
            pltpu.VMEM(matrices.shape, matrices.dtype),
            pltpu.SemaphoreType.DMA((2,)),
        ],
        compiler_params=params(),
        name="spectral_step",
    )(chunks, matrices, twiddle, *propagators, early)


def wavenumber(index):
    signed = jnp.where(index < SIZE // 2, index, index - SIZE).astype(jnp.float32)
    return signed * (2.0 * math.pi / (SIZE * grid_step))


def propagator_tables(angular, strip):
    block = strip % (2 * RADIX)
    lane = jnp.arange(2 * HALF, dtype=jnp.int32) % HALF
    column = block // 2 + RADIX * ((block % 2) * HALF + lane)
    wave_y = wavenumber(column)[None, None, :]
    row = (
        jnp.arange(RADIX, dtype=jnp.int32)[:, None]
        + RADIX * jnp.arange(INNER, dtype=jnp.int32)[None, :]
    )
    wave_x = wavenumber(row)[:, :, None]
    vertical_sq = angular * angular - wave_x * wave_x - wave_y * wave_y
    vertical = jnp.sqrt(jnp.abs(vertical_sq))
    propagating = vertical_sq > 0
    sine, cosine = sine_cosine(depth_step * vertical)
    real_part = jnp.where(propagating, cosine, jnp.exp(-depth_step * vertical))
    imag_part = jnp.where(propagating, sine, 0.0)
    sign = jnp.where(jnp.arange(2 * HALF) < HALF, -1.0, 1.0).astype(jnp.float32)
    return real_part, imag_part * sign[None, None, :]


def per_device(source_field, recorded, phase_index, slowness, slice_index):
    group = lax.axis_index(("xh", "c"))
    freq = lax.axis_index("zh")
    freqs = lax.axis_size("zh")
    encode_angle = lax.dynamic_slice_in_dim(phase_index, group, 1, 2)[0, :, 0].astype(
        jnp.float32
    ) * (2.0 * math.pi / PHASES)
    turn = jnp.stack([jnp.cos(encode_angle), jnp.sin(encode_angle)])
    angular = 0.5 + 1.5 * (freq.astype(jnp.float32) + 0.5) / freqs

    right = jnp.asarray(np.stack(lane_tables()))
    left = jnp.asarray(np.stack(row_tables()))
    lane_twiddle = jnp.asarray(lane_twiddles())
    row_twiddle = jnp.asarray(row_twiddles())
    slab = ("xh", "c", "zl", "y", "xl")
    propagators = propagator_tables(angular, lax.axis_index(slab))
    scaled = (depth_step * angular)[None]

    part_rows = ROWS // 2 // freqs
    parts = jnp.concatenate(
        [
            lax.dynamic_slice(
                slowness, (slice_index[d], group * part_rows, 0), (1, part_rows, SIZE)
            )
            for d in range(DEPTHS)
        ]
    )
    slow = lax.all_gather(parts, "zh", axis=0, tiled=False)

    chunks = first_step(turn, source_field, recorded, right, lane_twiddle, parts)
    chunks = lax.all_to_all(chunks, ("xh", "c"), 0, 0, tiled=True)
    chunks = lax.all_to_all(chunks, ("zh", "zl", "y", "xl"), 0, 0, tiled=True)
    pictures = []
    for descent in range(DEPTHS):
        last = descent == DEPTHS - 1
        chunks = spectral_step(
            chunks, left, row_twiddle, propagators, slow, descent > 0
        )
        chunks = lax.all_to_all(chunks, slab, 0, 0, tiled=True)
        result = space_step(
            scaled, chunks, slow, right, lane_twiddle, slow, descent, last
        )
        pictures.append(result[-1])
        if not last:
            chunks = lax.all_to_all(result[0], slab, 0, 0, tiled=True)
    picture = jnp.stack(pictures, axis=2)
    picture = picture.reshape((freqs * freqs,) + picture.shape[2:])
    picture = lax.all_to_all(picture, ("zh", "xh", "c"), 0, 0, tiled=True)
    picture = jnp.sum(picture.reshape((freqs, freqs) + picture.shape[1:]), axis=0)
    return picture.transpose(1, 0, 2, 3).reshape(DEPTHS, ROWS // 2, SIZE // freqs)


def solution(mesh):
    fine = Mesh(mesh.devices.reshape(2, 2, 4, 2, 4, 2), ("xh", "c", "zh", "zl", "y", "xl"))
    freq, strip = ("xh", "c"), ("zh", "zl", "y", "xl")
    placed = (
        P(None, freq, None, strip, None),
        P(None, freq, None, strip, None),
        P(),
        P(None, strip, None),
        P(),
    )
    return jax.shard_map(
        per_device, mesh=fine, in_specs=placed, out_specs=P(None, strip, freq), check_vma=False
    )
```

```python
import functools
import math

import jax
import jax.numpy as jnp
import numpy as np
from jax import lax
from jax.experimental import pallas as pl
from jax.experimental.pallas import tpu as pltpu
from jax.sharding import Mesh
from jax.sharding import PartitionSpec as P

DEPTHS = 4
PHASES = 8
SIZE = 2048
RADIX = 16
INNER = SIZE // RADIX
HALF = 64
ROWS = 64
VMEM_LIMIT = 12 * 1024 * 1024
FIRST_VMEM_LIMIT = 56 * 1024 * 1024

grid_step = 4.0
depth_step = 8.0


def split_table(table):
    high = table.astype(jnp.bfloat16)
    low = (table - high.astype(np.float64)).astype(jnp.bfloat16)
    return high, low


def inner_dft(direction):
    index = np.arange(INNER)
    angle = direction * 2.0 * np.pi * (np.outer(index, index) % INNER) / INNER
    return np.cos(angle), np.sin(angle)


def lane_tables():
    cosine, sine = inner_dft(-1.0)
    real_columns = np.concatenate([cosine, -sine], axis=0)
    imag_columns = np.concatenate([sine, cosine], axis=0)
    forward = np.concatenate(
        [
            part[:, half * HALF : (half + 1) * HALF]
            for half in range(2)
            for part in (real_columns, imag_columns)
        ],
        axis=1,
    )
    cosine, sine = inner_dft(1.0)
    real_rows = np.concatenate([cosine, sine], axis=1)
    imag_rows = np.concatenate([-sine, cosine], axis=1)
    inverse = (
        np.concatenate(
            [
                part[half * HALF : (half + 1) * HALF]
                for half in range(2)
                for part in (real_rows, imag_rows)
            ],
            axis=0,
        )
        / SIZE
    )
    out = []
    for table in (forward, inverse):
        high, low = split_table(table)
        out.append(np.concatenate([high, low, high], axis=0))
    return out


def row_tables():
    out = []
    for direction, scale in ((-1.0, 1.0), (1.0, 1.0 / SIZE)):
        cosine, sine = inner_dft(direction)
        high, low = split_table(np.concatenate([cosine, sine], axis=0) * scale)
        out.append(np.concatenate([high, low, high], axis=1))
    return out


def twiddles():
    angle = -2.0 * np.pi * np.outer(np.arange(RADIX), np.arange(INNER)) / SIZE
    return np.cos(angle), np.sin(angle)


def lane_twiddles():
    cosine, sine = twiddles()
    return np.concatenate([cosine, sine], axis=1).astype(np.float32)


def row_twiddles():
    cosine, sine = twiddles()
    sign = np.where(np.arange(2 * HALF) < HALF, -1.0, 1.0)
    return np.stack(
        [cosine[:, :, None] * np.ones(2 * HALF), sine[:, :, None] * sign]
    ).astype(np.float32)


def butterfly16(values, direction, add, sub, turn, scale_by):
    def four(a, b, c, d):
        even_sum, even_diff = add(a, c), sub(a, c)
        odd_sum, odd_diff = add(b, d), turn(sub(b, d), direction)
        return [
            add(even_sum, odd_sum),
            add(even_diff, odd_diff),
            sub(even_sum, odd_sum),
            sub(even_diff, odd_diff),
        ]

    first = [four(*[values[4 * n + m] for n in range(4)]) for m in range(4)]
    result = [None] * 16
    for k in range(4):
        column = []
        for m in range(4):
            value = first[m][k]
            power = m * k
            if power == 4:
                value = turn(value, direction)
            elif power:
                angle = direction * 2.0 * math.pi * power / 16
                value = scale_by(value, math.cos(angle), math.sin(angle))
            column.append(value)
        for m, value in enumerate(four(*column)):
            result[k + 4 * m] = value
    return result


def pair_add(a, b):
    return (a[0] + b[0], a[1] + b[1])


def pair_sub(a, b):
    return (a[0] - b[0], a[1] - b[1])


def pair_turn(a, s):
    return (-a[1], a[0]) if s > 0 else (a[1], -a[0])


def pair_scale(a, c, s):
    return (a[0] * c - a[1] * s, a[0] * s + a[1] * c)


def swap_halves(value):
    return pltpu.roll(value, HALF, 1)


def half_sign():
    lane = lax.broadcasted_iota(jnp.int32, (8, 2 * HALF), 1)
    return jnp.where(lane < HALF, -1.0, 1.0).astype(jnp.float32)


def split_value(value):
    high = value.astype(jnp.bfloat16)
    low = (value - high.astype(jnp.float32)).astype(jnp.bfloat16)
    return high, low


def sine_cosine(angle):
    turns = jnp.round(angle * (2.0 / math.pi))
    rest = angle - turns * 1.5703125
    rest = rest - turns * 4.8375129699707031e-4
    rest = rest - turns * 7.5497899548918821e-8
    square = rest * rest
    sine = rest + rest * square * (
        -1.6666654611e-1 + square * (8.3321608736e-3 - square * 1.9515295891e-4)
    )
    cosine = (
        1.0
        - 0.5 * square
        + square
        * square
        * (4.166664568298827e-2 + square * (-1.388731625493765e-3 + square * 2.443315711809948e-5))
    )
    quarter = turns.astype(jnp.int32)
    odd = (quarter & 1) == 1
    sine_out = jnp.where(odd, cosine, sine)
    cosine_out = jnp.where(odd, sine, cosine)
    sine_out = jnp.where((quarter & 2) == 2, -sine_out, sine_out)
    cosine_out = jnp.where(((quarter + 1) & 2) == 2, -cosine_out, cosine_out)
    return sine_out, cosine_out


def lanes(a):
    return slice(a * INNER, (a + 1) * INNER)


def forward_rows(wave, work, table, twiddle, out):
    @pl.loop(0, ROWS // 8)
    def _(tile):
        rows = pl.ds(tile * 8, 8)
        values = [(wave[0, rows, lanes(a)], wave[1, rows, lanes(a)]) for a in range(RADIX)]
        values = butterfly16(values, -1.0, pair_add, pair_sub, pair_turn, pair_scale)
        for k, (real, imag) in enumerate(values):
            if k:
                cosine = twiddle[k : k + 1, :INNER]
                sine = twiddle[k : k + 1, INNER:]
                real, imag = real * cosine - imag * sine, real * sine + imag * cosine
            work[k, rows, :INNER] = real
            work[k, rows, INNER:] = imag

    for group in range(0, RADIX, 4):
        value = work[group : group + 4].reshape(4 * ROWS, 2 * INNER)
        high, low = split_value(value)
        result = jnp.dot(
            jnp.concatenate([high, high, low], axis=1),
            table[...],
            preferred_element_type=jnp.float32,
        )
        result = result.reshape(4, ROWS, 2 * INNER)
        for k in range(4):
            for kind in range(2):
                for half in range(2):
                    out[(kind * RADIX + group + k) * 2 + half] = result[
                        k,
                        kind * (ROWS // 2) : (kind + 1) * (ROWS // 2),
                        half * INNER : (half + 1) * INNER,
                    ]


def inverse_rows(chunks, work, table, twiddle, wave):
    for group in range(0, RADIX, 4):
        parts = []
        for k in range(4):
            for kind in range(2):
                place = (kind * RADIX + group + k) * 2
                parts.append(jnp.concatenate([chunks[place], chunks[place + 1]], axis=1))
        high, low = split_value(jnp.concatenate(parts, axis=0))
        result = jnp.dot(
            jnp.concatenate([high, high, low], axis=1),
            table[...],
            preferred_element_type=jnp.float32,
        )
        work[group : group + 4] = result.reshape(4, ROWS, 2 * INNER)

    @pl.loop(0, ROWS // 8)
    def _(tile):
        rows = pl.ds(tile * 8, 8)
        values = []
        for k in range(RADIX):
            real, imag = work[k, rows, :INNER], work[k, rows, INNER:]
            if k:
                cosine = twiddle[k : k + 1, :INNER]
                sine = twiddle[k : k + 1, INNER:]
                real, imag = real * cosine + imag * sine, imag * cosine - real * sine
            values.append((real, imag))
        values = butterfly16(values, 1.0, pair_add, pair_sub, pair_turn, pair_scale)
        for a, (real, imag) in enumerate(values):
            wave[0, rows, lanes(a)] = real
            wave[1, rows, lanes(a)] = imag


def rotate_and_image(wave, slow, freq, angular, image, keep):
    half_rows = ROWS // 2
    strips, part_rows = slow.shape[:2]
    width = image.shape[3]

    @pl.loop(0, strips)
    def _(turn):
        strip = lax.rem(freq + strips - turn, strips)
        first = pl.ds(pl.multiple_of(strip * part_rows, part_rows), part_rows)
        second = pl.ds(pl.multiple_of(half_rows + strip * part_rows, part_rows), part_rows)
        for a in range(SIZE // 512):
            columns = slice(a * 512, (a + 1) * 512)
            sine, cosine = sine_cosine(angular * (slow[turn, :, columns] - 1.0))
            turned = []
            for rows in (first, second):
                real, imag = wave[0, rows, columns], wave[1, rows, columns]
                real, imag = real * cosine - imag * sine, real * sine + imag * cosine
                if keep:
                    wave[0, rows, columns] = real
                    wave[1, rows, columns] = imag
                turned.append((real, imag))
            picture = turned[0][0] * turned[1][0] - turned[0][1] * turned[1][1]
            place = a * 512 // width
            offset = a * 512 % width
            image[strip, place, :, offset : offset + 512] = picture * (1.0 / strips)


def fetch(pairs, semaphores):
    copies = [
        pltpu.make_async_copy(source, target, semaphores.at[n])
        for n, (source, target) in enumerate(pairs)
    ]
    for copy in copies:
        copy.start()
    return copies


def first_kernel(
    phases,
    places,
    turns,
    source,
    recorded,
    table,
    twiddle,
    slowness,
    out,
    parts,
    wave,
    work,
    fields,
    tables,
    factors,
    semaphores,
):
    half_rows = ROWS // 2
    group = lax.axis_index("xh") * lax.axis_size("c") + lax.axis_index("c")
    part_rows = parts.shape[1]
    part = pl.ds(pl.multiple_of(group * part_rows, part_rows), part_rows)
    copies = fetch(
        [
            (source, fields.at[0]),
            (recorded, fields.at[1]),
            (table, tables),
            (twiddle, factors),
        ]
        + [(slowness.at[places[d], part], parts.at[d]) for d in range(DEPTHS)],
        semaphores,
    )
    shots = fields.shape[1]
    levels = [phases[0, shot, group] & (PHASES - 1) for shot in range(shots)]
    angles = [(turns[0, level], turns[1, level]) for level in levels]
    for kind in range(2):
        copies[kind].wait()

        @pl.loop(0, half_rows // 16)
        def _(tile):
            rows = pl.ds(tile * 16, 16)
            place = pl.ds(kind * half_rows + tile * 16, 16)
            for a in range(SIZE // 512):
                columns = slice(a * 512, (a + 1) * 512)
                real_sum, imag_sum = None, None
                for shot in range(shots):
                    real = fields[kind, shot, 0, 0, rows, columns].astype(jnp.float32)
                    imag = fields[kind, shot, 0, 1, rows, columns].astype(jnp.float32)
                    cosine, sine = angles[shot]
                    real_part = cosine * real - sine * imag
                    imag_part = cosine * imag + sine * real
                    real_sum = real_part if real_sum is None else real_sum + real_part
                    imag_sum = imag_part if imag_sum is None else imag_sum + imag_part
                wave[0, place, columns] = real_sum
                wave[1, place, columns] = imag_sum if kind == 0 else -imag_sum

    for copy in copies[2:4]:
        copy.wait()
    forward_rows(wave, work, tables, factors, out)
    for copy in copies[4:]:
        copy.wait()


def space_kernel(depth, last, chunks, inverse_table, table, twiddle, *refs):
    strips = 4
    slow, refs = refs[:strips], refs[strips:]
    if last:
        image, wave, work, slow_here, semaphores = refs
    else:
        out, image, wave, work, slow_here, semaphores = refs
    copies = fetch([(slow[n].at[depth], slow_here.at[n]) for n in range(strips)], semaphores)
    freq = lax.axis_index("zh")
    angular = depth_step * (0.5 + 1.5 * (freq.astype(jnp.float32) + 0.5) / strips)
    inverse_rows(chunks, work, inverse_table, twiddle, wave)
    for copy in copies:
        copy.wait()
    rotate_and_image(wave, slow_here, freq, angular, image, not last)
    if not last:
        forward_rows(wave, work, table, twiddle, out)


WAVE = pltpu.VMEM((2, ROWS, SIZE), jnp.float32)
WORK = pltpu.VMEM((RADIX, ROWS, 2 * INNER), jnp.float32)
CHUNKS = jax.ShapeDtypeStruct((64, ROWS // 2, 2 * HALF), jnp.float32)


def whole():
    return pl.BlockSpec(memory_space=pltpu.VMEM)


def anywhere():
    return pl.BlockSpec(memory_space=pl.ANY)


def scalars():
    return pl.BlockSpec(memory_space=pltpu.SMEM)


def params():
    return pltpu.CompilerParams(vmem_limit_bytes=VMEM_LIMIT)


def first_step(phases, places, source, recorded, table, twiddle, slowness):
    angle = np.arange(PHASES) * (2.0 * np.pi / PHASES)
    turns = jnp.asarray(np.stack([np.cos(angle), np.sin(angle)]).astype(np.float32))
    part_rows = ROWS // 2 // phases.shape[2]
    return pl.pallas_call(
        first_kernel,
        out_shape=[
            CHUNKS,
            jax.ShapeDtypeStruct((DEPTHS, part_rows, SIZE), jnp.float32),
        ],
        in_specs=[scalars()] * 3 + [anywhere()] * 5,
        out_specs=[whole(), whole()],
        scratch_shapes=[
            WAVE,
            WORK,
            pltpu.VMEM((2,) + source.shape, source.dtype),
            pltpu.VMEM(table.shape, table.dtype),
            pltpu.VMEM(twiddle.shape, twiddle.dtype),
            pltpu.SemaphoreType.DMA((4 + DEPTHS,)),
        ],
        compiler_params=pltpu.CompilerParams(vmem_limit_bytes=FIRST_VMEM_LIMIT),
        name="encode_forward",
    )(phases, places, turns, source, recorded, table, twiddle, slowness)


def space_step(chunks, slow, tables, twiddle, depth, last):
    parts = len(slow)
    part = slow[0].shape[1:]
    image = jax.ShapeDtypeStruct((parts, parts, part[0], SIZE // parts), jnp.float32)
    out_shape = [image] if last else [CHUNKS, image]
    return pl.pallas_call(
        functools.partial(space_kernel, depth, last),
        out_shape=out_shape,
        in_specs=[whole()] * 4 + [anywhere()] * parts,
        out_specs=[whole()] * len(out_shape),
        scratch_shapes=[
            WAVE,
            WORK,
            pltpu.VMEM((parts,) + part, jnp.float32),
            pltpu.SemaphoreType.DMA((parts,)),
        ],
        compiler_params=params(),
        name="space_last" if last else "space_step",
    )(chunks, tables[1], tables[0], twiddle, *slow)


def spectral_kernel(
    slab_in, chunks, left, left_inverse, twiddle, prop_a, prop_b, out, work
):
    sign = half_sign()

    def turn(value, direction):
        return swap_halves(value) * (sign if direction > 0 else -sign)

    def scale_by(value, c, s):
        return value * c + swap_halves(value) * (sign * s)

    def add(a, b):
        return a + b

    def sub(a, b):
        return a - b

    tile_rows = 8

    def place(slab, a, tile):
        strip, part = a * (INNER // 32) + tile // 4, tile % 4
        if slab:
            return part * 16 + strip % 16, strip // 16 * 8
        return strip, part * 8

    def turn_rows(value, k, rows, direction):
        turned = swap_halves(value) * twiddle[1, k, rows]
        value = value * twiddle[0, k, rows]
        return value - turned if direction > 0 else value + turned

    for tile in range(INNER // tile_rows):
        rows = slice(tile * tile_rows, (tile + 1) * tile_rows)
        values = []
        for a in range(RADIX):
            chunk, row = place(slab_in, a, tile)
            values.append(chunks[chunk, row : row + tile_rows, :])
        values = butterfly16(values, -1.0, add, sub, turn, scale_by)
        for k, value in enumerate(values):
            if k:
                value = turn_rows(value, k, rows, -1.0)
            work[k, rows] = value

    wide_sign = jnp.concatenate([sign, sign], axis=1)[:1]

    def multiply(matrix, value):
        high, low = split_value(value)
        result = jnp.dot(
            matrix[...],
            jnp.concatenate([high, high, low], axis=0),
            preferred_element_type=jnp.float32,
        )
        swapped = jnp.concatenate(
            [swap_halves(result[INNER:, :INNER]), swap_halves(result[INNER:, INNER:])], axis=1
        )
        return result[:INNER] + swapped * wide_sign

    for pair in range(0, RADIX, 2):
        value = jnp.concatenate([work[pair], work[pair + 1]], axis=1)
        value = multiply(left, value)
        shifted = []
        for k in range(2):
            part = value[:, k * INNER : (k + 1) * INNER]
            shifted.append(part * prop_a[pair + k] + swap_halves(part) * prop_b[pair + k])
        value = multiply(left_inverse, jnp.concatenate(shifted, axis=1))
        work[pair] = value[:, :INNER]
        work[pair + 1] = value[:, INNER:]

    for tile in range(INNER // tile_rows):
        rows = slice(tile * tile_rows, (tile + 1) * tile_rows)
        values = []
        for k in range(RADIX):
            value = work[k, rows]
            if k:
                value = turn_rows(value, k, rows, 1.0)
            values.append(value)
        values = butterfly16(values, 1.0, add, sub, turn, scale_by)
        for a, value in enumerate(values):
            chunk, row = place(True, a, tile)
            out[chunk, row : row + tile_rows, :] = value


def spectral_step(chunks, matrices, twiddle, propagators, slab_in):
    return pl.pallas_call(
        functools.partial(spectral_kernel, slab_in),
        out_shape=CHUNKS,
        in_specs=[whole()] * 6,
        out_specs=whole(),
        scratch_shapes=[pltpu.VMEM((RADIX, INNER, 2 * HALF), jnp.float32)],
        compiler_params=params(),
        name="spectral_step",
    )(chunks, *matrices, twiddle, *propagators)


def wavenumber(index):
    signed = jnp.where(index < SIZE // 2, index, index - SIZE).astype(jnp.float32)
    return signed * (2.0 * math.pi / (SIZE * grid_step))


def propagator_tables(angular, strip):
    block = strip % (2 * RADIX)
    lane = jnp.arange(2 * HALF, dtype=jnp.int32) % HALF
    column = block // 2 + RADIX * ((block % 2) * HALF + lane)
    wave_y = wavenumber(column)[None, None, :]
    row = (
        jnp.arange(RADIX, dtype=jnp.int32)[:, None]
        + RADIX * jnp.arange(INNER, dtype=jnp.int32)[None, :]
    )
    wave_x = wavenumber(row)[:, :, None]
    vertical_sq = angular * angular - wave_x * wave_x - wave_y * wave_y
    vertical = jnp.sqrt(jnp.abs(vertical_sq))
    propagating = vertical_sq > 0
    sine, cosine = sine_cosine(depth_step * vertical)
    real_part = jnp.where(propagating, cosine, jnp.exp(-depth_step * vertical))
    imag_part = jnp.where(propagating, sine, 0.0)
    sign = jnp.where(jnp.arange(2 * HALF) < HALF, -1.0, 1.0).astype(jnp.float32)
    return real_part, imag_part * sign[None, None, :]


def per_device(source_field, recorded, phase_index, slowness, slice_index):
    freq = lax.axis_index("zh")
    freqs = lax.axis_size("zh")
    angular = 0.5 + 1.5 * (freq.astype(jnp.float32) + 0.5) / freqs
    slab = ("xh", "c", "zl", "y", "xl")
    right = [jnp.asarray(t) for t in lane_tables()]
    left = [jnp.asarray(t) for t in row_tables()]
    lane_twiddle = jnp.asarray(lane_twiddles())
    row_twiddle = jnp.asarray(row_twiddles())
    propagators = propagator_tables(angular, lax.axis_index(slab))

    chunks, parts = first_step(
        phase_index, slice_index, source_field, recorded, right[0], lane_twiddle, slowness
    )
    slow = [parts]
    for step in range(1, freqs):
        ring = [(z, (z + step) % freqs) for z in range(freqs)]
        slow.append(lax.ppermute(parts, "zh", ring))
    chunks = lax.all_to_all(chunks, ("xh", "c"), 0, 0, tiled=True)
    chunks, slow = lax.optimization_barrier((chunks, slow))
    chunks = lax.all_to_all(chunks, ("zh", "zl", "y", "xl"), 0, 0, tiled=True)
    pictures = []
    for descent in range(DEPTHS):
        last = descent == DEPTHS - 1
        chunks = spectral_step(chunks, left, row_twiddle, propagators, descent > 0)
        chunks = lax.all_to_all(chunks, slab, 0, 0, tiled=True)
        result = space_step(chunks, slow, right, lane_twiddle, descent, last)
        pictures.append(result[-1])
        if not last:
            chunks = lax.all_to_all(result[0], slab, 0, 0, tiled=True)
    picture = jnp.stack(pictures, axis=2)
    picture = picture.reshape((freqs * freqs,) + picture.shape[2:])
    picture = lax.all_to_all(picture, ("zh", "xh", "c"), 0, 0, tiled=True)
    picture = jnp.sum(picture.reshape((freqs, freqs) + picture.shape[1:]), axis=0)
    return picture.transpose(1, 0, 2, 3).reshape(DEPTHS, ROWS // 2, SIZE // freqs)


def solution(mesh):
    fine = Mesh(mesh.devices.reshape(2, 2, 4, 2, 4, 2), ("xh", "c", "zh", "zl", "y", "xl"))
    freq, strip = ("xh", "c"), ("zh", "zl", "y", "xl")
    placed = (
        P(None, freq, None, strip, None),
        P(None, freq, None, strip, None),
        P(),
        P(None, strip, None),
        P(),
    )
    return jax.shard_map(
        per_device, mesh=fine, in_specs=placed, out_specs=P(None, strip, freq), check_vma=False
    )
```

```python
import functools
import math

import jax
import jax.numpy as jnp
import numpy as np
from jax import lax
from jax.experimental import pallas as pl
from jax.experimental.pallas import tpu as pltpu
from jax.sharding import Mesh
from jax.sharding import PartitionSpec as P

DEPTHS = 4
PHASES = 8
SIZE = 2048
RADIX = 16
HALF_RADIX = RADIX // 2
INNER = SIZE // RADIX
HALF = 64
ROWS = 64
VMEM_LIMIT = 12 * 1024 * 1024
FIRST_VMEM_LIMIT = 56 * 1024 * 1024

grid_step = 4.0
depth_step = 8.0


def split_table(table):
    high = table.astype(jnp.bfloat16)
    low = (table - high.astype(np.float64)).astype(jnp.bfloat16)
    return high, low


def inner_dft(direction):
    index = np.arange(INNER)
    angle = direction * 2.0 * np.pi * (np.outer(index, index) % INNER) / INNER
    return np.cos(angle), np.sin(angle)


def lane_tables():
    cosine, sine = inner_dft(-1.0)
    real_columns = np.concatenate([cosine, -sine], axis=0)
    imag_columns = np.concatenate([sine, cosine], axis=0)
    forward = np.concatenate(
        [
            part[:, half * HALF : (half + 1) * HALF]
            for half in range(2)
            for part in (real_columns, imag_columns)
        ],
        axis=1,
    )
    cosine, sine = inner_dft(1.0)
    real_rows = np.concatenate([cosine, sine], axis=1)
    imag_rows = np.concatenate([-sine, cosine], axis=1)
    inverse = (
        np.concatenate(
            [
                part[half * HALF : (half + 1) * HALF]
                for half in range(2)
                for part in (real_rows, imag_rows)
            ],
            axis=0,
        )
        / SIZE
    )
    out = []
    for table in (forward, inverse):
        high, low = split_table(table)
        out.append(np.concatenate([high, low, high], axis=0))
    return out


def row_tables():
    out = []
    for direction, scale in ((-1.0, 1.0), (1.0, 1.0 / SIZE)):
        cosine, sine = inner_dft(direction)
        table = np.concatenate(
            [np.concatenate([cosine, -sine], axis=1), np.concatenate([sine, cosine], axis=1)]
        )
        high, low = split_table(table * scale)
        out.append(np.concatenate([high, low, high], axis=1))
    return out


def lane_twiddles():
    angle = -2.0 * np.pi * np.outer(np.arange(RADIX), np.arange(INNER)) / SIZE
    factors = np.concatenate([np.cos(angle), np.sin(angle)], axis=1)
    return np.broadcast_to(factors[:, None], (RADIX, 8, 2 * INNER)).astype(np.float32)


def row_twiddles():
    odd = (np.arange(2 * HALF) >= HALF).astype(np.int64)
    order = 2 * np.arange(HALF_RADIX)[:, None, None] + odd
    angle = -2.0 * np.pi * (order * np.arange(INNER)[None, :, None]) / SIZE
    return np.stack([np.cos(angle), np.sin(angle)]).astype(np.float32)


def add(a, b):
    return (a[0] + b[0], a[1] + b[1])


def sub(a, b):
    return (a[0] - b[0], a[1] - b[1])


def turn(a, s):
    return (-a[1], a[0]) if s > 0 else (a[1], -a[0])


def scale(a, c, s):
    return (a[0] * c - a[1] * s, a[0] * s + a[1] * c)


def butterfly4(a, b, c, d, direction):
    even_sum, even_diff = add(a, c), sub(a, c)
    odd_sum, odd_diff = add(b, d), turn(sub(b, d), direction)
    return [
        add(even_sum, odd_sum),
        add(even_diff, odd_diff),
        sub(even_sum, odd_sum),
        sub(even_diff, odd_diff),
    ]


def butterfly8(values, direction):
    even = butterfly4(*values[0::2], direction)
    odd = butterfly4(*values[1::2], direction)
    root = math.sqrt(0.5)

    def eighth(a):
        if direction > 0:
            return ((a[0] - a[1]) * root, (a[0] + a[1]) * root)
        return ((a[0] + a[1]) * root, (a[1] - a[0]) * root)

    odd[1] = eighth(odd[1])
    odd[2] = turn(odd[2], direction)
    odd[3] = turn(eighth(odd[3]), direction)
    return [add(e, o) for e, o in zip(even, odd)] + [sub(e, o) for e, o in zip(even, odd)]


def butterfly16(values, direction):
    first = [butterfly4(*values[m::4], direction) for m in range(4)]
    result = [None] * 16
    for k in range(4):
        column = []
        for m in range(4):
            value = first[m][k]
            power = m * k
            if power == 4:
                value = turn(value, direction)
            elif power:
                angle = direction * 2.0 * math.pi * power / 16
                value = scale(value, math.cos(angle), math.sin(angle))
            column.append(value)
        for m, value in enumerate(butterfly4(*column, direction)):
            result[k + 4 * m] = value
    return result


def swap_halves(value):
    return pltpu.roll(value, HALF, 1)


def split_value(value):
    high = value.astype(jnp.bfloat16)
    low = (value - high.astype(jnp.float32)).astype(jnp.bfloat16)
    return high, low


def sine_cosine(angle):
    turns = jnp.round(angle * (2.0 / math.pi))
    rest = angle - turns * 1.5703125
    rest = rest - turns * 4.8375129699707031e-4
    rest = rest - turns * 7.5497899548918821e-8
    square = rest * rest
    sine = rest + rest * square * (
        -1.6666654611e-1 + square * (8.3321608736e-3 - square * 1.9515295891e-4)
    )
    cosine = (
        1.0
        - 0.5 * square
        + square
        * square
        * (4.166664568298827e-2 + square * (-1.388731625493765e-3 + square * 2.443315711809948e-5))
    )
    quarter = turns.astype(jnp.int32)
    odd = (quarter & 1) == 1
    sine_out = jnp.where(odd, cosine, sine)
    cosine_out = jnp.where(odd, sine, cosine)
    sine_out = jnp.where((quarter & 2) == 2, -sine_out, sine_out)
    cosine_out = jnp.where(((quarter + 1) & 2) == 2, -cosine_out, cosine_out)
    return sine_out, cosine_out


def lanes(a):
    return slice(a * INNER, (a + 1) * INNER)


def forward_rows(wave, work, table, twiddle, out):
    @pl.loop(0, ROWS // 8)
    def _(tile):
        rows = pl.ds(tile * 8, 8)
        values = [(wave[0, rows, lanes(a)], wave[1, rows, lanes(a)]) for a in range(RADIX)]
        values = butterfly16(values, -1.0)
        for k, (real, imag) in enumerate(values):
            if k:
                cosine = twiddle[k, :, :INNER]
                sine = twiddle[k, :, INNER:]
                real, imag = real * cosine - imag * sine, real * sine + imag * cosine
            work[k, rows, :INNER] = real
            work[k, rows, INNER:] = imag

    for group in range(0, RADIX, 4):
        value = work[group : group + 4].reshape(4 * ROWS, 2 * INNER)
        high, low = split_value(value)
        result = jnp.dot(
            jnp.concatenate([high, high, low], axis=1),
            table[...],
            preferred_element_type=jnp.float32,
        )
        result = result.reshape(4, ROWS, 2 * INNER)
        for k in range(4):
            for kind in range(2):
                for half in range(2):
                    out[(kind * RADIX + group + k) * 2 + half] = result[
                        k,
                        kind * (ROWS // 2) : (kind + 1) * (ROWS // 2),
                        half * INNER : (half + 1) * INNER,
                    ]


def inverse_rows(chunks, work, table, twiddle, wave):
    for group in range(0, RADIX, 4):
        parts = []
        for k in range(4):
            for kind in range(2):
                place = (kind * RADIX + group + k) * 2
                parts.append(jnp.concatenate([chunks[place], chunks[place + 1]], axis=1))
        high, low = split_value(jnp.concatenate(parts, axis=0))
        result = jnp.dot(
            jnp.concatenate([high, high, low], axis=1),
            table[...],
            preferred_element_type=jnp.float32,
        )
        work[group : group + 4] = result.reshape(4, ROWS, 2 * INNER)

    @pl.loop(0, ROWS // 8)
    def _(tile):
        rows = pl.ds(tile * 8, 8)
        values = []
        for k in range(RADIX):
            real, imag = work[k, rows, :INNER], work[k, rows, INNER:]
            if k:
                cosine = twiddle[k, :, :INNER]
                sine = twiddle[k, :, INNER:]
                real, imag = real * cosine + imag * sine, imag * cosine - real * sine
            values.append((real, imag))
        values = butterfly16(values, 1.0)
        for a, (real, imag) in enumerate(values):
            wave[0, rows, lanes(a)] = real
            wave[1, rows, lanes(a)] = imag


def rotate_and_image(wave, slow, freq, angular, image, keep):
    half_rows = ROWS // 2
    strips, part_rows = slow.shape[:2]
    width = image.shape[3]

    @pl.loop(0, strips)
    def _(turn):
        strip = lax.rem(freq + strips - turn, strips)
        first = pl.ds(pl.multiple_of(strip * part_rows, part_rows), part_rows)
        second = pl.ds(pl.multiple_of(half_rows + strip * part_rows, part_rows), part_rows)
        for a in range(SIZE // 512):
            columns = slice(a * 512, (a + 1) * 512)
            sine, cosine = sine_cosine(angular * (slow[turn, :, columns] - 1.0))
            turned = []
            for rows in (first, second):
                real, imag = wave[0, rows, columns], wave[1, rows, columns]
                real, imag = real * cosine - imag * sine, real * sine + imag * cosine
                if keep:
                    wave[0, rows, columns] = real
                    wave[1, rows, columns] = imag
                turned.append((real, imag))
            picture = turned[0][0] * turned[1][0] - turned[0][1] * turned[1][1]
            place = a * 512 // width
            offset = a * 512 % width
            image[strip, place, :, offset : offset + 512] = picture * (1.0 / strips)


def fetch(pairs, semaphores):
    copies = [
        pltpu.make_async_copy(source, target, semaphores.at[n])
        for n, (source, target) in enumerate(pairs)
    ]
    for copy in copies:
        copy.start()
    return copies


def first_kernel(
    phases,
    places,
    turns,
    source,
    recorded,
    table,
    twiddle,
    slowness,
    out,
    parts,
    wave,
    work,
    fields,
    tables,
    factors,
    semaphores,
):
    half_rows = ROWS // 2
    group = lax.axis_index("xh") * lax.axis_size("c") + lax.axis_index("c")
    part_rows = parts.shape[1]
    part = pl.ds(pl.multiple_of(group * part_rows, part_rows), part_rows)
    copies = fetch(
        [
            (source, fields.at[0]),
            (recorded, fields.at[1]),
            (table, tables),
            (twiddle, factors),
        ]
        + [(slowness.at[places[d], part], parts.at[d]) for d in range(DEPTHS)],
        semaphores,
    )
    shots = fields.shape[1]
    levels = [phases[0, shot, group] & (PHASES - 1) for shot in range(shots)]
    angles = [(turns[0, level], turns[1, level]) for level in levels]
    for kind in range(2):
        copies[kind].wait()

        @pl.loop(0, half_rows // 16)
        def _(tile):
            rows = pl.ds(tile * 16, 16)
            place = pl.ds(kind * half_rows + tile * 16, 16)
            for a in range(SIZE // 512):
                columns = slice(a * 512, (a + 1) * 512)
                real_sum, imag_sum = None, None
                for shot in range(shots):
                    real = fields[kind, shot, 0, 0, rows, columns].astype(jnp.float32)
                    imag = fields[kind, shot, 0, 1, rows, columns].astype(jnp.float32)
                    cosine, sine = angles[shot]
                    real_part = cosine * real - sine * imag
                    imag_part = cosine * imag + sine * real
                    real_sum = real_part if real_sum is None else real_sum + real_part
                    imag_sum = imag_part if imag_sum is None else imag_sum + imag_part
                wave[0, place, columns] = real_sum
                wave[1, place, columns] = imag_sum if kind == 0 else -imag_sum

    for copy in copies[2:4]:
        copy.wait()
    forward_rows(wave, work, tables, factors, out)
    for copy in copies[4:]:
        copy.wait()


def space_kernel(places, last, chunks, inverse_table, table, twiddle, *refs):
    strips = 4
    slow, refs = refs[:strips], refs[strips:]
    if last:
        image, wave, work, slow_here, semaphores = refs
    else:
        out, image, wave, work, slow_here, semaphores = refs
    copies = fetch([(slow[n].at[places[n]], slow_here.at[n]) for n in range(strips)], semaphores)
    freq = lax.axis_index("zh")
    angular = depth_step * (0.5 + 1.5 * (freq.astype(jnp.float32) + 0.5) / strips)
    inverse_rows(chunks, work, inverse_table, twiddle, wave)
    for copy in copies:
        copy.wait()
    rotate_and_image(wave, slow_here, freq, angular, image, not last)
    if not last:
        forward_rows(wave, work, table, twiddle, out)


WAVE = pltpu.VMEM((2, ROWS, SIZE), jnp.float32)
WORK = pltpu.VMEM((RADIX, ROWS, 2 * INNER), jnp.float32)
CHUNKS = jax.ShapeDtypeStruct((64, ROWS // 2, 2 * HALF), jnp.float32)


def whole():
    return pl.BlockSpec(memory_space=pltpu.VMEM)


def anywhere():
    return pl.BlockSpec(memory_space=pl.ANY)


def scalars():
    return pl.BlockSpec(memory_space=pltpu.SMEM)


def params():
    return pltpu.CompilerParams(vmem_limit_bytes=VMEM_LIMIT)


def first_step(phases, places, source, recorded, table, twiddle, slowness):
    angle = np.arange(PHASES) * (2.0 * np.pi / PHASES)
    turns = jnp.asarray(np.stack([np.cos(angle), np.sin(angle)]).astype(np.float32))
    part_rows = ROWS // 2 // phases.shape[2]
    return pl.pallas_call(
        first_kernel,
        out_shape=[
            CHUNKS,
            jax.ShapeDtypeStruct((DEPTHS, part_rows, SIZE), jnp.float32),
        ],
        in_specs=[scalars()] * 3 + [anywhere()] * 5,
        out_specs=[whole(), whole()],
        scratch_shapes=[
            WAVE,
            WORK,
            pltpu.VMEM((2,) + source.shape, source.dtype),
            pltpu.VMEM(table.shape, table.dtype),
            pltpu.VMEM(twiddle.shape, twiddle.dtype),
            pltpu.SemaphoreType.DMA((4 + DEPTHS,)),
        ],
        compiler_params=pltpu.CompilerParams(vmem_limit_bytes=FIRST_VMEM_LIMIT),
        name="encode_forward",
    )(phases, places, turns, source, recorded, table, twiddle, slowness)


def space_step(chunks, slow, tables, twiddle, last):
    slow, places = zip(*slow)
    parts = len(slow)
    part = slow[0].shape[1:]
    image = jax.ShapeDtypeStruct((parts, parts, part[0], SIZE // parts), jnp.float32)
    out_shape = [image] if last else [CHUNKS, image]
    return pl.pallas_call(
        functools.partial(space_kernel, places, last),
        out_shape=out_shape,
        in_specs=[whole()] * 4 + [anywhere()] * parts,
        out_specs=[whole()] * len(out_shape),
        scratch_shapes=[
            WAVE,
            WORK,
            pltpu.VMEM((parts,) + part, jnp.float32),
            pltpu.SemaphoreType.DMA((parts,)),
        ],
        compiler_params=params(),
        name="space_last" if last else "space_step",
    )(chunks, tables[1], tables[0], twiddle, *slow)


def spectral_kernel(
    slab_in, chunks, left, left_inverse, twiddle, prop_real, prop_imag, out, work
):
    tile_rows = 8
    tiles = INNER // tile_rows
    low_half = lax.broadcasted_iota(jnp.int32, (tile_rows, 2 * HALF), 1) < HALF

    def place(slab, tile):
        strip, part = tile // 4, tile % 4
        if slab:
            return part * 16 + strip % 16, strip // 16 * tile_rows
        return strip, part * tile_rows

    def odd_factor(a):
        angle = -2.0 * math.pi * a / RADIX
        return (
            jnp.where(low_half, 1.0, math.cos(angle)).astype(jnp.float32),
            jnp.where(low_half, 0.0, math.sin(angle)).astype(jnp.float32),
        )

    factors = [odd_factor(a) for a in range(HALF_RADIX)]

    for tile in range(tiles):
        rows = slice(tile * tile_rows, (tile + 1) * tile_rows)
        imag_rows = slice(INNER + tile * tile_rows, INNER + (tile + 1) * tile_rows)
        values = []
        for a in range(HALF_RADIX):
            pair = []
            for half in range(2):
                chunk, row = place(slab_in, (half * HALF_RADIX + a) * tiles + tile)
                pair.append(chunks[chunk, row : row + tile_rows, :])
            total, rest = pair[0] + pair[1], pair[0] - pair[1]
            value = (
                jnp.where(low_half, total, swap_halves(rest)),
                jnp.where(low_half, swap_halves(total), rest),
            )
            values.append(scale(value, *factors[a]) if a else value)
        for k, value in enumerate(butterfly8(values, -1.0)):
            real, imag = scale(value, twiddle[0, k, rows], twiddle[1, k, rows])
            work[k, rows] = real
            work[k, imag_rows] = imag

    def multiply(matrix, value):
        high, low = split_value(value)
        return jnp.dot(
            matrix[...],
            jnp.concatenate([high, high, low], axis=0),
            preferred_element_type=jnp.float32,
        )

    for pair in range(0, HALF_RADIX, 2):
        value = multiply(left, jnp.concatenate([work[pair], work[pair + 1]], axis=1))
        factor = [
            jnp.concatenate([table[pair], table[pair + 1]], axis=1)
            for table in (prop_real, prop_imag)
        ]
        value = jnp.concatenate(scale((value[:INNER], value[INNER:]), *factor), axis=0)
        value = multiply(left_inverse, value)
        work[pair] = value[:, :INNER]
        work[pair + 1] = value[:, INNER:]

    for tile in range(tiles):
        rows = slice(tile * tile_rows, (tile + 1) * tile_rows)
        imag_rows = slice(INNER + tile * tile_rows, INNER + (tile + 1) * tile_rows)
        values = [
            scale((work[k, rows], work[k, imag_rows]), twiddle[0, k, rows], -twiddle[1, k, rows])
            for k in range(HALF_RADIX)
        ]
        for a, value in enumerate(butterfly8(values, 1.0)):
            if a:
                value = scale(value, factors[a][0], -factors[a][1])
            real, imag = value
            total = jnp.where(low_half, real, swap_halves(imag))
            rest = jnp.where(low_half, swap_halves(real), imag)
            for half, result in enumerate((total + rest, total - rest)):
                chunk, row = place(True, (half * HALF_RADIX + a) * tiles + tile)
                out[chunk, row : row + tile_rows, :] = result


def spectral_step(chunks, matrices, twiddle, propagators, slab_in):
    return pl.pallas_call(
        functools.partial(spectral_kernel, slab_in),
        out_shape=CHUNKS,
        in_specs=[whole()] * 6,
        out_specs=whole(),
        scratch_shapes=[pltpu.VMEM((HALF_RADIX, 2 * INNER, 2 * HALF), jnp.float32)],
        compiler_params=params(),
        name="spectral_step",
    )(chunks, *matrices, twiddle, *propagators)


def wavenumber(index):
    signed = jnp.where(index < SIZE // 2, index, index - SIZE).astype(jnp.float32)
    return signed * (2.0 * math.pi / (SIZE * grid_step))


def propagator_tables(angular, block):
    lane = jnp.arange(2 * HALF, dtype=jnp.int32)
    column = block // 2 + RADIX * ((block % 2) * HALF + lane % HALF)
    wave_y = wavenumber(column)[None, None, :]
    row = (
        jnp.arange(HALF_RADIX, dtype=jnp.int32)[:, None, None]
        + HALF_RADIX * jnp.arange(INNER, dtype=jnp.int32)[None, :, None]
    )
    wave_x = wavenumber(2 * row + lane // HALF)
    vertical_sq = angular * angular - wave_x * wave_x - wave_y * wave_y
    vertical = jnp.sqrt(jnp.abs(vertical_sq))
    propagating = vertical_sq > 0
    sine, cosine = sine_cosine(depth_step * vertical)
    real_part = jnp.where(propagating, cosine, jnp.exp(-depth_step * vertical))
    imag_part = jnp.where(propagating, sine, 0.0)
    return real_part, imag_part


def per_device(source_field, recorded, phase_index, slowness, slice_index):
    freq = lax.axis_index("zh")
    freqs = lax.axis_size("zh")
    angular = 0.5 + 1.5 * (freq.astype(jnp.float32) + 0.5) / freqs
    slab = ("xh", "c", "zl", "y", "xl")
    right = [jnp.asarray(t) for t in lane_tables()]
    left = [jnp.asarray(t) for t in row_tables()]
    lane_twiddle = jnp.asarray(lane_twiddles())
    row_twiddle = jnp.asarray(row_twiddles())
    propagators = propagator_tables(angular, lax.axis_index(slab) % (2 * RADIX))

    chunks, parts = first_step(
        phase_index, slice_index, source_field, recorded, right[0], lane_twiddle, slowness
    )
    up = [(z, (z + 1) % freqs) for z in range(freqs)]
    down = [(z, (z - 1) % freqs) for z in range(freqs)]
    middle = DEPTHS // 2
    below = lax.ppermute(parts, "zh", up)
    above = lax.ppermute(parts, "zh", down)
    chunks = lax.all_to_all(chunks, ("xh", "c"), 0, 0, tiled=True)
    chunks, below, above = lax.optimization_barrier((chunks, below, above))
    far = [
        lax.ppermute(below[:middle], "zh", up),
        lax.ppermute(above[middle:], "zh", down),
    ]
    chunks = lax.all_to_all(chunks, ("zh", "zl", "y", "xl"), 0, 0, tiled=True)
    chunks, far = lax.optimization_barrier((chunks, far))
    pictures = []
    for descent in range(DEPTHS):
        last = descent == DEPTHS - 1
        chunks = spectral_step(chunks, left, row_twiddle, propagators, descent > 0)
        chunks = lax.all_to_all(chunks, slab, 0, 0, tiled=True)
        late, at = divmod(descent, middle)
        slow = [(parts, descent), (below, descent), (far[late], at), (above, descent)]
        result = space_step(chunks, slow, right, lane_twiddle, last)
        pictures.append(result[-1])
        if not last:
            chunks = lax.all_to_all(result[0], slab, 0, 0, tiled=True)
    picture = jnp.stack(pictures, axis=2)
    picture = picture.reshape((freqs * freqs,) + picture.shape[2:])
    picture = lax.all_to_all(picture, ("zh", "xh", "c"), 0, 0, tiled=True)
    picture = jnp.sum(picture.reshape((freqs, freqs) + picture.shape[1:]), axis=0)
    return picture.transpose(1, 0, 2, 3).reshape(DEPTHS, ROWS // 2, SIZE // freqs)


def solution(mesh):
    fine = Mesh(mesh.devices.reshape(2, 2, 4, 2, 4, 2), ("xh", "c", "zh", "zl", "y", "xl"))
    freq, strip = ("xh", "c"), ("zh", "zl", "y", "xl")
    placed = (
        P(None, freq, None, strip, None),
        P(None, freq, None, strip, None),
        P(),
        P(None, strip, None),
        P(),
    )
    return jax.shard_map(
        per_device, mesh=fine, in_specs=placed, out_specs=P(None, strip, freq), check_vma=False
    )
```

```python
import functools
import math

import jax
import jax.numpy as jnp
import numpy as np
from jax import lax
from jax.experimental import pallas as pl
from jax.experimental.pallas import tpu as pltpu
from jax.sharding import Mesh
from jax.sharding import PartitionSpec as P

DEPTHS = 4
PHASES = 8
SIZE = 2048
RADIX = 16
HALF_RADIX = RADIX // 2
INNER = SIZE // RADIX
HALF = 64
ROWS = 64
VMEM_LIMIT = 12 * 1024 * 1024
FIRST_VMEM_LIMIT = 56 * 1024 * 1024

grid_step = 4.0
depth_step = 8.0


def split_table(table):
    high = table.astype(jnp.bfloat16)
    low = (table - high.astype(np.float64)).astype(jnp.bfloat16)
    return high, low


def inner_dft(direction):
    index = np.arange(INNER)
    angle = direction * 2.0 * np.pi * (np.outer(index, index) % INNER) / INNER
    return np.cos(angle), np.sin(angle)


def lane_tables():
    cosine, sine = inner_dft(-1.0)
    real_columns = np.concatenate([cosine, -sine], axis=0)
    imag_columns = np.concatenate([sine, cosine], axis=0)
    forward = np.concatenate(
        [
            part[:, half * HALF : (half + 1) * HALF]
            for half in range(2)
            for part in (real_columns, imag_columns)
        ],
        axis=1,
    )
    cosine, sine = inner_dft(1.0)
    real_rows = np.concatenate([cosine, sine], axis=1)
    imag_rows = np.concatenate([-sine, cosine], axis=1)
    inverse = (
        np.concatenate(
            [
                part[half * HALF : (half + 1) * HALF]
                for half in range(2)
                for part in (real_rows, imag_rows)
            ],
            axis=0,
        )
        / SIZE
    )
    out = []
    for table in (forward, inverse):
        high, low = split_table(table)
        out.append(np.concatenate([high, low, high], axis=0))
    return out


def row_tables():
    out = []
    for direction, scale in ((-1.0, 1.0), (1.0, 1.0 / SIZE)):
        cosine, sine = inner_dft(direction)
        table = np.concatenate(
            [np.concatenate([cosine, -sine], axis=1), np.concatenate([sine, cosine], axis=1)]
        )
        high, low = split_table(table * scale)
        out.append(np.concatenate([high, low, high], axis=1))
    return out


def lane_twiddles():
    angle = -2.0 * np.pi * np.outer(np.arange(RADIX), np.arange(INNER)) / SIZE
    factors = np.concatenate([np.cos(angle), np.sin(angle)], axis=1)
    return np.broadcast_to(factors[:, None], (RADIX, 8, 2 * INNER)).astype(np.float32)


def row_twiddles():
    odd = (np.arange(2 * HALF) >= HALF).astype(np.int64)
    order = 2 * np.arange(HALF_RADIX)[:, None, None] + odd
    angle = -2.0 * np.pi * (order * np.arange(INNER)[None, :, None]) / SIZE
    return np.stack([np.cos(angle), np.sin(angle)]).astype(np.float32)


def add(a, b):
    return (a[0] + b[0], a[1] + b[1])


def sub(a, b):
    return (a[0] - b[0], a[1] - b[1])


def turn(a, s):
    return (-a[1], a[0]) if s > 0 else (a[1], -a[0])


def scale(a, c, s):
    return (a[0] * c - a[1] * s, a[0] * s + a[1] * c)


def butterfly4(a, b, c, d, direction):
    even_sum, even_diff = add(a, c), sub(a, c)
    odd_sum, odd_diff = add(b, d), turn(sub(b, d), direction)
    return [
        add(even_sum, odd_sum),
        add(even_diff, odd_diff),
        sub(even_sum, odd_sum),
        sub(even_diff, odd_diff),
    ]


def butterfly8(values, direction):
    even = butterfly4(*values[0::2], direction)
    odd = butterfly4(*values[1::2], direction)
    root = math.sqrt(0.5)

    def eighth(a):
        if direction > 0:
            return ((a[0] - a[1]) * root, (a[0] + a[1]) * root)
        return ((a[0] + a[1]) * root, (a[1] - a[0]) * root)

    odd[1] = eighth(odd[1])
    odd[2] = turn(odd[2], direction)
    odd[3] = turn(eighth(odd[3]), direction)
    return [add(e, o) for e, o in zip(even, odd)] + [sub(e, o) for e, o in zip(even, odd)]


def butterfly16(values, direction):
    first = [butterfly4(*values[m::4], direction) for m in range(4)]
    result = [None] * 16
    for k in range(4):
        column = []
        for m in range(4):
            value = first[m][k]
            power = m * k
            if power == 4:
                value = turn(value, direction)
            elif power:
                angle = direction * 2.0 * math.pi * power / 16
                value = scale(value, math.cos(angle), math.sin(angle))
            column.append(value)
        for m, value in enumerate(butterfly4(*column, direction)):
            result[k + 4 * m] = value
    return result


def swap_halves(value):
    return pltpu.roll(value, HALF, 1)


def split_value(value):
    high = value.astype(jnp.bfloat16)
    low = (value - high.astype(jnp.float32)).astype(jnp.bfloat16)
    return high, low


def sine_cosine(angle):
    turns = jnp.round(angle * (2.0 / math.pi))
    rest = angle - turns * 1.5703125
    rest = rest - turns * 4.8375129699707031e-4
    rest = rest - turns * 7.5497899548918821e-8
    square = rest * rest
    sine = rest + rest * square * (
        -1.6666654611e-1 + square * (8.3321608736e-3 - square * 1.9515295891e-4)
    )
    cosine = (
        1.0
        - 0.5 * square
        + square
        * square
        * (4.166664568298827e-2 + square * (-1.388731625493765e-3 + square * 2.443315711809948e-5))
    )
    quarter = turns.astype(jnp.int32)
    odd = (quarter & 1) == 1
    sine_out = jnp.where(odd, cosine, sine)
    cosine_out = jnp.where(odd, sine, cosine)
    sine_out = jnp.where((quarter & 2) == 2, -sine_out, sine_out)
    cosine_out = jnp.where(((quarter + 1) & 2) == 2, -cosine_out, cosine_out)
    return sine_out, cosine_out


def lanes(a):
    return slice(a * INNER, (a + 1) * INNER)


def forward_rows(wave, work, table, twiddle, out):
    for tile in range(ROWS // 8):
        rows = slice(tile * 8, tile * 8 + 8)
        values = [(wave[0, rows, lanes(a)], wave[1, rows, lanes(a)]) for a in range(RADIX)]
        values = butterfly16(values, -1.0)
        for k, (real, imag) in enumerate(values):
            if k:
                cosine = twiddle[k, :, :INNER]
                sine = twiddle[k, :, INNER:]
                real, imag = real * cosine - imag * sine, real * sine + imag * cosine
            work[k, rows, :INNER] = real
            work[k, rows, INNER:] = imag

    for group in range(0, RADIX, 4):
        value = work[group : group + 4].reshape(4 * ROWS, 2 * INNER)
        high, low = split_value(value)
        result = jnp.dot(
            jnp.concatenate([high, high, low], axis=1),
            table[...],
            preferred_element_type=jnp.float32,
        )
        result = result.reshape(4, ROWS, 2 * INNER)
        for k in range(4):
            for kind in range(2):
                for half in range(2):
                    out[(kind * RADIX + group + k) * 2 + half] = result[
                        k,
                        kind * (ROWS // 2) : (kind + 1) * (ROWS // 2),
                        half * INNER : (half + 1) * INNER,
                    ]


def inverse_rows(chunks, work, table, twiddle, wave):
    for group in range(0, RADIX, 4):
        parts = []
        for k in range(4):
            for kind in range(2):
                place = (kind * RADIX + group + k) * 2
                parts.append(jnp.concatenate([chunks[place], chunks[place + 1]], axis=1))
        high, low = split_value(jnp.concatenate(parts, axis=0))
        result = jnp.dot(
            jnp.concatenate([high, high, low], axis=1),
            table[...],
            preferred_element_type=jnp.float32,
        )
        work[group : group + 4] = result.reshape(4, ROWS, 2 * INNER)

    for tile in range(ROWS // 8):
        rows = slice(tile * 8, tile * 8 + 8)
        values = []
        for k in range(RADIX):
            real, imag = work[k, rows, :INNER], work[k, rows, INNER:]
            if k:
                cosine = twiddle[k, :, :INNER]
                sine = twiddle[k, :, INNER:]
                real, imag = real * cosine + imag * sine, imag * cosine - real * sine
            values.append((real, imag))
        values = butterfly16(values, 1.0)
        for a, (real, imag) in enumerate(values):
            wave[0, rows, lanes(a)] = real
            wave[1, rows, lanes(a)] = imag


def rotate_and_image(wave, slow, places, freq, angular, image, keep):
    half_rows = ROWS // 2
    strips, part_rows = image.shape[0], image.shape[2]
    width = image.shape[3]

    for turn in range(strips):
        strip = lax.rem(freq + strips - turn, strips)
        first = pl.ds(pl.multiple_of(strip * part_rows, part_rows), part_rows)
        second = pl.ds(pl.multiple_of(half_rows + strip * part_rows, part_rows), part_rows)
        for a in range(SIZE // 512):
            columns = slice(a * 512, (a + 1) * 512)
            sine, cosine = sine_cosine(angular * (slow[turn][places[turn], :, columns] - 1.0))
            turned = []
            for rows in (first, second):
                real, imag = wave[0, rows, columns], wave[1, rows, columns]
                real, imag = real * cosine - imag * sine, real * sine + imag * cosine
                if keep:
                    wave[0, rows, columns] = real
                    wave[1, rows, columns] = imag
                turned.append((real, imag))
            picture = turned[0][0] * turned[1][0] - turned[0][1] * turned[1][1]
            place = a * 512 // width
            offset = a * 512 % width
            image[strip, place, :, offset : offset + 512] = picture * (1.0 / strips)


def fetch(pairs, semaphores):
    copies = [
        pltpu.make_async_copy(source, target, semaphores.at[n])
        for n, (source, target) in enumerate(pairs)
    ]
    for copy in copies:
        copy.start()
    return copies


def first_kernel(
    phases,
    places,
    turns,
    source,
    recorded,
    table,
    twiddle,
    slowness,
    out,
    parts,
    wave,
    work,
    fields,
    tables,
    factors,
    semaphores,
):
    half_rows = ROWS // 2
    group = lax.axis_index("xh") * lax.axis_size("c") + lax.axis_index("c")
    part_rows = parts.shape[1]
    part = pl.ds(pl.multiple_of(group * part_rows, part_rows), part_rows)
    copies = fetch(
        [
            (source, fields.at[0]),
            (recorded, fields.at[1]),
            (table, tables),
            (twiddle, factors),
        ]
        + [(slowness.at[places[d], part], parts.at[d]) for d in range(DEPTHS)],
        semaphores,
    )
    shots = fields.shape[1]
    levels = [phases[0, shot, group] & (PHASES - 1) for shot in range(shots)]
    angles = [(turns[0, level], turns[1, level]) for level in levels]
    for kind in range(2):
        copies[kind].wait()

        for tile in range(half_rows // 16):
            rows = slice(tile * 16, tile * 16 + 16)
            place = slice(kind * half_rows + tile * 16, kind * half_rows + tile * 16 + 16)
            for a in range(SIZE // 512):
                columns = slice(a * 512, (a + 1) * 512)
                real_sum, imag_sum = None, None
                for shot in range(shots):
                    real = fields[kind, shot, 0, 0, rows, columns].astype(jnp.float32)
                    imag = fields[kind, shot, 0, 1, rows, columns].astype(jnp.float32)
                    cosine, sine = angles[shot]
                    real_part = cosine * real - sine * imag
                    imag_part = cosine * imag + sine * real
                    real_sum = real_part if real_sum is None else real_sum + real_part
                    imag_sum = imag_part if imag_sum is None else imag_sum + imag_part
                wave[0, place, columns] = real_sum
                wave[1, place, columns] = imag_sum if kind == 0 else -imag_sum

    for copy in copies[2:4]:
        copy.wait()
    forward_rows(wave, work, tables, factors, out)
    for copy in copies[4:]:
        copy.wait()


def space_kernel(places, last, chunks, inverse_table, table, twiddle, *refs):
    strips = len(places)
    slow, refs = refs[:strips], refs[strips:]
    if last:
        image, wave, work = refs
    else:
        out, image, wave, work = refs
    freq = lax.axis_index("zh")
    angular = depth_step * (0.5 + 1.5 * (freq.astype(jnp.float32) + 0.5) / strips)
    inverse_rows(chunks, work, inverse_table, twiddle, wave)
    rotate_and_image(wave, slow, places, freq, angular, image, not last)
    if not last:
        forward_rows(wave, work, table, twiddle, out)


WAVE = pltpu.VMEM((2, ROWS, SIZE), jnp.float32)
WORK = pltpu.VMEM((RADIX, ROWS, 2 * INNER), jnp.float32)
CHUNKS = jax.ShapeDtypeStruct((64, ROWS // 2, 2 * HALF), jnp.float32)


def whole():
    return pl.BlockSpec(memory_space=pltpu.VMEM)


def anywhere():
    return pl.BlockSpec(memory_space=pl.ANY)


def scalars():
    return pl.BlockSpec(memory_space=pltpu.SMEM)


def params():
    return pltpu.CompilerParams(vmem_limit_bytes=VMEM_LIMIT)


def first_step(phases, places, source, recorded, table, twiddle, slowness):
    angle = np.arange(PHASES) * (2.0 * np.pi / PHASES)
    turns = jnp.asarray(np.stack([np.cos(angle), np.sin(angle)]).astype(np.float32))
    part_rows = ROWS // 2 // phases.shape[2]
    return pl.pallas_call(
        first_kernel,
        out_shape=[
            CHUNKS,
            jax.ShapeDtypeStruct((DEPTHS, part_rows, SIZE), jnp.float32),
        ],
        in_specs=[scalars()] * 3 + [anywhere()] * 5,
        out_specs=[whole(), whole()],
        scratch_shapes=[
            WAVE,
            WORK,
            pltpu.VMEM((2,) + source.shape, source.dtype),
            pltpu.VMEM(table.shape, table.dtype),
            pltpu.VMEM(twiddle.shape, twiddle.dtype),
            pltpu.SemaphoreType.DMA((4 + DEPTHS,)),
        ],
        compiler_params=pltpu.CompilerParams(vmem_limit_bytes=FIRST_VMEM_LIMIT),
        name="encode_forward",
    )(phases, places, turns, source, recorded, table, twiddle, slowness)


def space_step(chunks, slow, tables, twiddle, last):
    slow, places = zip(*slow)
    parts = len(slow)
    part = slow[0].shape[1:]
    image = jax.ShapeDtypeStruct((parts, parts, part[0], SIZE // parts), jnp.float32)
    out_shape = [image] if last else [CHUNKS, image]
    return pl.pallas_call(
        functools.partial(space_kernel, places, last),
        out_shape=out_shape,
        in_specs=[whole()] * (4 + parts),
        out_specs=[whole()] * len(out_shape),
        scratch_shapes=[
            WAVE,
            WORK,
        ],
        compiler_params=params(),
        name="space_last" if last else "space_step",
    )(chunks, tables[1], tables[0], twiddle, *slow)


def spectral_kernel(
    slab_in, chunks, left, left_inverse, twiddle, prop_real, prop_imag, out, work
):
    tile_rows = 8
    tiles = INNER // tile_rows
    low_half = lax.broadcasted_iota(jnp.int32, (tile_rows, 2 * HALF), 1) < HALF

    def place(slab, tile):
        strip, part = tile // 4, tile % 4
        if slab:
            return part * 16 + strip % 16, strip // 16 * tile_rows
        return strip, part * tile_rows

    def odd_factor(a):
        angle = -2.0 * math.pi * a / RADIX
        return (
            jnp.where(low_half, 1.0, math.cos(angle)).astype(jnp.float32),
            jnp.where(low_half, 0.0, math.sin(angle)).astype(jnp.float32),
        )

    factors = [odd_factor(a) for a in range(HALF_RADIX)]

    for tile in range(tiles):
        rows = slice(tile * tile_rows, (tile + 1) * tile_rows)
        imag_rows = slice(INNER + tile * tile_rows, INNER + (tile + 1) * tile_rows)
        values = []
        for a in range(HALF_RADIX):
            pair = []
            for half in range(2):
                chunk, row = place(slab_in, (half * HALF_RADIX + a) * tiles + tile)
                pair.append(chunks[chunk, row : row + tile_rows, :])
            total, rest = pair[0] + pair[1], pair[0] - pair[1]
            value = (
                jnp.where(low_half, total, swap_halves(rest)),
                jnp.where(low_half, swap_halves(total), rest),
            )
            values.append(scale(value, *factors[a]) if a else value)
        for k, value in enumerate(butterfly8(values, -1.0)):
            real, imag = scale(value, twiddle[0, k, rows], twiddle[1, k, rows])
            work[k, rows] = real
            work[k, imag_rows] = imag

    def multiply(matrix, value):
        high, low = split_value(value)
        return jnp.dot(
            matrix[...],
            jnp.concatenate([high, high, low], axis=0),
            preferred_element_type=jnp.float32,
        )

    for pair in range(0, HALF_RADIX, 2):
        value = multiply(left, jnp.concatenate([work[pair], work[pair + 1]], axis=1))
        factor = [
            jnp.concatenate([table[pair], table[pair + 1]], axis=1)
            for table in (prop_real, prop_imag)
        ]
        value = jnp.concatenate(scale((value[:INNER], value[INNER:]), *factor), axis=0)
        value = multiply(left_inverse, value)
        work[pair] = value[:, :INNER]
        work[pair + 1] = value[:, INNER:]

    for tile in range(tiles):
        rows = slice(tile * tile_rows, (tile + 1) * tile_rows)
        imag_rows = slice(INNER + tile * tile_rows, INNER + (tile + 1) * tile_rows)
        values = [
            scale((work[k, rows], work[k, imag_rows]), twiddle[0, k, rows], -twiddle[1, k, rows])
            for k in range(HALF_RADIX)
        ]
        for a, value in enumerate(butterfly8(values, 1.0)):
            if a:
                value = scale(value, factors[a][0], -factors[a][1])
            real, imag = value
            total = jnp.where(low_half, real, swap_halves(imag))
            rest = jnp.where(low_half, swap_halves(real), imag)
            for half, result in enumerate((total + rest, total - rest)):
                chunk, row = place(True, (half * HALF_RADIX + a) * tiles + tile)
                out[chunk, row : row + tile_rows, :] = result


def spectral_step(chunks, matrices, twiddle, propagators, slab_in):
    return pl.pallas_call(
        functools.partial(spectral_kernel, slab_in),
        out_shape=CHUNKS,
        in_specs=[whole()] * 6,
        out_specs=whole(),
        scratch_shapes=[pltpu.VMEM((HALF_RADIX, 2 * INNER, 2 * HALF), jnp.float32)],
        compiler_params=params(),
        name="spectral_step",
    )(chunks, *matrices, twiddle, *propagators)


def wavenumber(index):
    signed = jnp.where(index < SIZE // 2, index, index - SIZE).astype(jnp.float32)
    return signed * (2.0 * math.pi / (SIZE * grid_step))


def propagator_tables(angular, block):
    lane = jnp.arange(2 * HALF, dtype=jnp.int32)
    column = block // 2 + RADIX * ((block % 2) * HALF + lane % HALF)
    wave_y = wavenumber(column)[None, None, :]
    row = (
        jnp.arange(HALF_RADIX, dtype=jnp.int32)[:, None, None]
        + HALF_RADIX * jnp.arange(INNER, dtype=jnp.int32)[None, :, None]
    )
    wave_x = wavenumber(2 * row + lane // HALF)
    vertical_sq = angular * angular - wave_x * wave_x - wave_y * wave_y
    vertical = jnp.sqrt(jnp.abs(vertical_sq))
    propagating = vertical_sq > 0
    sine, cosine = sine_cosine(depth_step * vertical)
    real_part = jnp.where(propagating, cosine, jnp.exp(-depth_step * vertical))
    imag_part = jnp.where(propagating, sine, 0.0)
    return real_part, imag_part


def per_device(source_field, recorded, phase_index, slowness, slice_index):
    freq = lax.axis_index("zh")
    freqs = lax.axis_size("zh")
    angular = 0.5 + 1.5 * (freq.astype(jnp.float32) + 0.5) / freqs
    slab = ("xh", "c", "zl", "y", "xl")
    right = [jnp.asarray(t) for t in lane_tables()]
    left = [jnp.asarray(t) for t in row_tables()]
    lane_twiddle = jnp.asarray(lane_twiddles())
    row_twiddle = jnp.asarray(row_twiddles())
    propagators = propagator_tables(angular, lax.axis_index(slab) % (2 * RADIX))

    chunks, parts = first_step(
        phase_index, slice_index, source_field, recorded, right[0], lane_twiddle, slowness
    )
    up = [(z, (z + 1) % freqs) for z in range(freqs)]
    down = [(z, (z - 1) % freqs) for z in range(freqs)]
    middle = DEPTHS // 2
    below = lax.ppermute(parts, "zh", up)
    above = lax.ppermute(parts, "zh", down)
    chunks = lax.all_to_all(chunks, ("xh", "c"), 0, 0, tiled=True)
    chunks, below, above = lax.optimization_barrier((chunks, below, above))
    far = [
        lax.ppermute(below[:middle], "zh", up),
        lax.ppermute(above[middle:], "zh", down),
    ]
    chunks = lax.all_to_all(chunks, ("zh", "zl", "y", "xl"), 0, 0, tiled=True)
    chunks, far = lax.optimization_barrier((chunks, far))
    pictures = []
    for descent in range(DEPTHS):
        last = descent == DEPTHS - 1
        chunks = spectral_step(chunks, left, row_twiddle, propagators, descent > 0)
        chunks = lax.all_to_all(chunks, slab, 0, 0, tiled=True)
        late, at = divmod(descent, middle)
        slow = [(parts, descent), (below, descent), (far[late], at), (above, descent)]
        result = space_step(chunks, slow, right, lane_twiddle, last)
        pictures.append(result[-1])
        if not last:
            chunks = lax.all_to_all(result[0], slab, 0, 0, tiled=True)
    picture = jnp.stack(pictures, axis=2)
    picture = picture.reshape((freqs * freqs,) + picture.shape[2:])
    picture = lax.all_to_all(picture, ("zh", "xh", "c"), 0, 0, tiled=True)
    picture = jnp.sum(picture.reshape((freqs, freqs) + picture.shape[1:]), axis=0)
    return picture.transpose(1, 0, 2, 3).reshape(DEPTHS, ROWS // 2, SIZE // freqs)


def solution(mesh):
    fine = Mesh(mesh.devices.reshape(2, 2, 4, 2, 4, 2), ("xh", "c", "zh", "zl", "y", "xl"))
    freq, strip = ("xh", "c"), ("zh", "zl", "y", "xl")
    placed = (
        P(None, freq, None, strip, None),
        P(None, freq, None, strip, None),
        P(),
        P(None, strip, None),
        P(),
    )
    return jax.shard_map(
        per_device, mesh=fine, in_specs=placed, out_specs=P(None, strip, freq), check_vma=False
    )
```

```python
import functools
import math

import jax
import jax.numpy as jnp
import numpy as np
from jax import lax
from jax.experimental import pallas as pl
from jax.experimental.pallas import tpu as pltpu
from jax.sharding import Mesh
from jax.sharding import PartitionSpec as P

DEPTHS = 4
PHASES = 8
SIZE = 2048
RADIX = 16
HALF_RADIX = RADIX // 2
INNER = SIZE // RADIX
HALF = 64
ROWS = 64
VMEM_LIMIT = 12 * 1024 * 1024
FIRST_VMEM_LIMIT = 56 * 1024 * 1024

grid_step = 4.0
depth_step = 8.0


def split_table(table):
    high = table.astype(jnp.bfloat16)
    low = (table - high.astype(np.float64)).astype(jnp.bfloat16)
    return high, low


def inner_dft(direction):
    index = np.arange(INNER)
    angle = direction * 2.0 * np.pi * (np.outer(index, index) % INNER) / INNER
    return np.cos(angle), np.sin(angle)


def lane_tables():
    cosine, sine = inner_dft(-1.0)
    real_columns = np.concatenate([cosine, -sine], axis=0)
    imag_columns = np.concatenate([sine, cosine], axis=0)
    forward = np.concatenate(
        [
            part[:, half * HALF : (half + 1) * HALF]
            for half in range(2)
            for part in (real_columns, imag_columns)
        ],
        axis=1,
    )
    cosine, sine = inner_dft(1.0)
    real_rows = np.concatenate([cosine, sine], axis=1)
    imag_rows = np.concatenate([-sine, cosine], axis=1)
    inverse = (
        np.concatenate(
            [
                part[half * HALF : (half + 1) * HALF]
                for half in range(2)
                for part in (real_rows, imag_rows)
            ],
            axis=0,
        )
        / SIZE
    )
    out = []
    for table in (forward, inverse):
        high, low = split_table(table)
        out.append(np.concatenate([high, low, high], axis=0))
    return out


def row_tables():
    out = []
    for direction, scale in ((-1.0, 1.0), (1.0, 1.0 / SIZE)):
        cosine, sine = inner_dft(direction)
        table = np.concatenate(
            [np.concatenate([cosine, -sine], axis=1), np.concatenate([sine, cosine], axis=1)]
        )
        high, low = split_table(table * scale)
        out.append(np.concatenate([high, low, high], axis=1))
    return out


def lane_twiddles():
    angle = -2.0 * np.pi * np.outer(np.arange(RADIX), np.arange(INNER)) / SIZE
    factors = np.concatenate([np.cos(angle), np.sin(angle)], axis=1)
    return np.broadcast_to(factors[:, None], (RADIX, 8, 2 * INNER)).astype(np.float32)


def row_twiddles():
    odd = (np.arange(2 * HALF) >= HALF).astype(np.int64)
    order = 2 * np.arange(HALF_RADIX)[:, None, None] + odd
    angle = -2.0 * np.pi * (order * np.arange(INNER)[None, :, None]) / SIZE
    return np.stack([np.cos(angle), np.sin(angle)]).astype(np.float32)


def add(a, b):
    return (a[0] + b[0], a[1] + b[1])


def sub(a, b):
    return (a[0] - b[0], a[1] - b[1])


def turn(a, s):
    return (-a[1], a[0]) if s > 0 else (a[1], -a[0])


def scale(a, c, s):
    return (a[0] * c - a[1] * s, a[0] * s + a[1] * c)


def butterfly4(a, b, c, d, direction):
    even_sum, even_diff = add(a, c), sub(a, c)
    odd_sum, odd_diff = add(b, d), turn(sub(b, d), direction)
    return [
        add(even_sum, odd_sum),
        add(even_diff, odd_diff),
        sub(even_sum, odd_sum),
        sub(even_diff, odd_diff),
    ]


def butterfly8(values, direction):
    even = butterfly4(*values[0::2], direction)
    odd = butterfly4(*values[1::2], direction)
    root = math.sqrt(0.5)

    def eighth(a):
        if direction > 0:
            return ((a[0] - a[1]) * root, (a[0] + a[1]) * root)
        return ((a[0] + a[1]) * root, (a[1] - a[0]) * root)

    odd[1] = eighth(odd[1])
    odd[2] = turn(odd[2], direction)
    odd[3] = turn(eighth(odd[3]), direction)
    return [add(e, o) for e, o in zip(even, odd)] + [sub(e, o) for e, o in zip(even, odd)]


def butterfly16(values, direction):
    first = [butterfly4(*values[m::4], direction) for m in range(4)]
    result = [None] * 16
    for k in range(4):
        column = []
        for m in range(4):
            value = first[m][k]
            power = m * k
            if power == 4:
                value = turn(value, direction)
            elif power:
                angle = direction * 2.0 * math.pi * power / 16
                value = scale(value, math.cos(angle), math.sin(angle))
            column.append(value)
        for m, value in enumerate(butterfly4(*column, direction)):
            result[k + 4 * m] = value
    return result


def swap_halves(value):
    return pltpu.roll(value, HALF, 1)


def split_value(value):
    high = value.astype(jnp.bfloat16)
    low = (value - high.astype(jnp.float32)).astype(jnp.bfloat16)
    return high, low


def sine_cosine(angle):
    turns = jnp.round(angle * (2.0 / math.pi))
    rest = angle - turns * 1.5703125
    rest = rest - turns * 4.8375129699707031e-4
    rest = rest - turns * 7.5497899548918821e-8
    square = rest * rest
    sine = rest + rest * square * (
        -1.6666654611e-1 + square * (8.3321608736e-3 - square * 1.9515295891e-4)
    )
    cosine = (
        1.0
        - 0.5 * square
        + square
        * square
        * (4.166664568298827e-2 + square * (-1.388731625493765e-3 + square * 2.443315711809948e-5))
    )
    quarter = turns.astype(jnp.int32)
    odd = (quarter & 1) == 1
    sine_out = jnp.where(odd, cosine, sine)
    cosine_out = jnp.where(odd, sine, cosine)
    sine_out = jnp.where((quarter & 2) == 2, -sine_out, sine_out)
    cosine_out = jnp.where(((quarter + 1) & 2) == 2, -cosine_out, cosine_out)
    return sine_out, cosine_out


def rotation(half_angle):
    square = half_angle * half_angle
    sine = 1.0 / 120.0 + square * (-1.0 / 5040.0 + square * (1.0 / 362880.0 - square * (1.0 / 39916800.0)))
    sine = half_angle * (1.0 + square * (-1.0 / 6.0 + square * sine))
    cosine = -1.0 / 720.0 + square * (
        1.0 / 40320.0 + square * (-1.0 / 3628800.0 + square * (1.0 / 479001600.0))
    )
    cosine = 1.0 + square * (-0.5 + square * (1.0 / 24.0 + square * cosine))
    double = sine + sine
    return double * cosine, 1.0 - double * sine


def lanes(a):
    return slice(a * INNER, (a + 1) * INNER)


def forward_rows(wave, work, table, twiddle, out):
    for tile in range(ROWS // 8):
        rows = slice(tile * 8, tile * 8 + 8)
        values = [(wave[0, rows, lanes(a)], wave[1, rows, lanes(a)]) for a in range(RADIX)]
        values = butterfly16(values, -1.0)
        for k, (real, imag) in enumerate(values):
            if k:
                cosine = twiddle[k, :, :INNER]
                sine = twiddle[k, :, INNER:]
                real, imag = real * cosine - imag * sine, real * sine + imag * cosine
            work[k, rows, :INNER] = real
            work[k, rows, INNER:] = imag

    for group in range(0, RADIX, 4):
        value = work[group : group + 4].reshape(4 * ROWS, 2 * INNER)
        high, low = split_value(value)
        result = jnp.dot(
            jnp.concatenate([high, high, low], axis=1),
            table[...],
            preferred_element_type=jnp.float32,
        )
        result = result.reshape(4, ROWS, 2 * INNER)
        for k in range(4):
            for kind in range(2):
                for half in range(2):
                    out[(kind * RADIX + group + k) * 2 + half] = result[
                        k,
                        kind * (ROWS // 2) : (kind + 1) * (ROWS // 2),
                        half * INNER : (half + 1) * INNER,
                    ]


def inverse_rows(chunks, work, table, twiddle, wave):
    for group in range(0, RADIX, 4):
        parts = []
        for k in range(4):
            for kind in range(2):
                place = (kind * RADIX + group + k) * 2
                parts.append(jnp.concatenate([chunks[place], chunks[place + 1]], axis=1))
        high, low = split_value(jnp.concatenate(parts, axis=0))
        result = jnp.dot(
            jnp.concatenate([high, high, low], axis=1),
            table[...],
            preferred_element_type=jnp.float32,
        )
        work[group : group + 4] = result.reshape(4, ROWS, 2 * INNER)

    for tile in range(ROWS // 8):
        rows = slice(tile * 8, tile * 8 + 8)
        values = []
        for k in range(RADIX):
            real, imag = work[k, rows, :INNER], work[k, rows, INNER:]
            if k:
                cosine = twiddle[k, :, :INNER]
                sine = twiddle[k, :, INNER:]
                real, imag = real * cosine + imag * sine, imag * cosine - real * sine
            values.append((real, imag))
        values = butterfly16(values, 1.0)
        for a, (real, imag) in enumerate(values):
            wave[0, rows, lanes(a)] = real
            wave[1, rows, lanes(a)] = imag


def rotate_and_image(wave, slow, places, freq, angular, image, keep):
    half_rows = ROWS // 2
    strips, part_rows = image.shape[0], image.shape[2]
    width = image.shape[3]
    half_angular = 0.5 * angular

    for turn in range(strips):
        strip = lax.rem(freq + strips - turn, strips)
        first = pl.ds(pl.multiple_of(strip * part_rows, part_rows), part_rows)
        second = pl.ds(pl.multiple_of(half_rows + strip * part_rows, part_rows), part_rows)
        for a in range(SIZE // 512):
            columns = slice(a * 512, (a + 1) * 512)
            sine, cosine = rotation(half_angular * (slow[turn][places[turn], :, columns] - 1.0))
            turned = []
            for rows in (first, second):
                real, imag = wave[0, rows, columns], wave[1, rows, columns]
                real, imag = real * cosine - imag * sine, real * sine + imag * cosine
                if keep:
                    wave[0, rows, columns] = real
                    wave[1, rows, columns] = imag
                turned.append((real, imag))
            picture = turned[0][0] * turned[1][0] - turned[0][1] * turned[1][1]
            place = a * 512 // width
            offset = a * 512 % width
            image[strip, place, :, offset : offset + 512] = picture * (1.0 / strips)


def fetch(pairs, semaphores):
    copies = [
        pltpu.make_async_copy(source, target, semaphores.at[n])
        for n, (source, target) in enumerate(pairs)
    ]
    for copy in copies:
        copy.start()
    return copies


def first_kernel(
    phases,
    places,
    turns,
    source,
    recorded,
    table,
    twiddle,
    slowness,
    out,
    parts,
    wave,
    work,
    fields,
    tables,
    factors,
    semaphores,
):
    half_rows = ROWS // 2
    group = lax.axis_index("xh") * lax.axis_size("c") + lax.axis_index("c")
    part_rows = parts.shape[1]
    part = pl.ds(pl.multiple_of(group * part_rows, part_rows), part_rows)
    copies = fetch(
        [
            (source, fields.at[0]),
            (recorded, fields.at[1]),
            (table, tables),
            (twiddle, factors),
        ]
        + [(slowness.at[places[d], part], parts.at[d]) for d in range(DEPTHS)],
        semaphores,
    )
    shots = fields.shape[1]
    levels = [phases[0, shot, group] & (PHASES - 1) for shot in range(shots)]
    angles = [(turns[0, level], turns[1, level]) for level in levels]
    for kind in range(2):
        copies[kind].wait()

        for tile in range(half_rows // 16):
            rows = slice(tile * 16, tile * 16 + 16)
            place = slice(kind * half_rows + tile * 16, kind * half_rows + tile * 16 + 16)
            for a in range(SIZE // 512):
                columns = slice(a * 512, (a + 1) * 512)
                real_sum, imag_sum = None, None
                for shot in range(shots):
                    real = fields[kind, shot, 0, 0, rows, columns].astype(jnp.float32)
                    imag = fields[kind, shot, 0, 1, rows, columns].astype(jnp.float32)
                    cosine, sine = angles[shot]
                    real_part = cosine * real - sine * imag
                    imag_part = cosine * imag + sine * real
                    real_sum = real_part if real_sum is None else real_sum + real_part
                    imag_sum = imag_part if imag_sum is None else imag_sum + imag_part
                wave[0, place, columns] = real_sum
                wave[1, place, columns] = imag_sum if kind == 0 else -imag_sum

    for copy in copies[2:4]:
        copy.wait()
    forward_rows(wave, work, tables, factors, out)
    for copy in copies[4:]:
        copy.wait()


def space_kernel(places, last, chunks, inverse_table, table, twiddle, *refs):
    strips = len(places)
    slow, refs = refs[:strips], refs[strips:]
    if last:
        image, wave, work = refs
    else:
        out, image, wave, work = refs
    freq = lax.axis_index("zh")
    angular = depth_step * (0.5 + 1.5 * (freq.astype(jnp.float32) + 0.5) / strips)
    inverse_rows(chunks, work, inverse_table, twiddle, wave)
    rotate_and_image(wave, slow, places, freq, angular, image, not last)
    if not last:
        forward_rows(wave, work, table, twiddle, out)


WAVE = pltpu.VMEM((2, ROWS, SIZE), jnp.float32)
WORK = pltpu.VMEM((RADIX, ROWS, 2 * INNER), jnp.float32)
CHUNKS = jax.ShapeDtypeStruct((64, ROWS // 2, 2 * HALF), jnp.float32)


def whole():
    return pl.BlockSpec(memory_space=pltpu.VMEM)


def anywhere():
    return pl.BlockSpec(memory_space=pl.ANY)


def scalars():
    return pl.BlockSpec(memory_space=pltpu.SMEM)


def params():
    return pltpu.CompilerParams(vmem_limit_bytes=VMEM_LIMIT)


def first_step(phases, places, source, recorded, table, twiddle, slowness):
    angle = np.arange(PHASES) * (2.0 * np.pi / PHASES)
    turns = jnp.asarray(np.stack([np.cos(angle), np.sin(angle)]).astype(np.float32))
    part_rows = ROWS // 2 // phases.shape[2]
    return pl.pallas_call(
        first_kernel,
        out_shape=[
            CHUNKS,
            jax.ShapeDtypeStruct((DEPTHS, part_rows, SIZE), jnp.float32),
        ],
        in_specs=[scalars()] * 3 + [anywhere()] * 5,
        out_specs=[whole(), whole()],
        scratch_shapes=[
            WAVE,
            WORK,
            pltpu.VMEM((2,) + source.shape, source.dtype),
            pltpu.VMEM(table.shape, table.dtype),
            pltpu.VMEM(twiddle.shape, twiddle.dtype),
            pltpu.SemaphoreType.DMA((4 + DEPTHS,)),
        ],
        compiler_params=pltpu.CompilerParams(vmem_limit_bytes=FIRST_VMEM_LIMIT),
        name="encode_forward",
    )(phases, places, turns, source, recorded, table, twiddle, slowness)


def space_step(chunks, slow, tables, twiddle, last):
    slow, places = zip(*slow)
    parts = len(slow)
    part = slow[0].shape[1:]
    image = jax.ShapeDtypeStruct((parts, parts, part[0], SIZE // parts), jnp.float32)
    out_shape = [image] if last else [CHUNKS, image]
    return pl.pallas_call(
        functools.partial(space_kernel, places, last),
        out_shape=out_shape,
        in_specs=[whole()] * (4 + parts),
        out_specs=[whole()] * len(out_shape),
        scratch_shapes=[
            WAVE,
            WORK,
        ],
        compiler_params=params(),
        name="space_last" if last else "space_step",
    )(chunks, tables[1], tables[0], twiddle, *slow)


def spectral_kernel(
    slab_in, chunks, left, left_inverse, twiddle, prop_real, prop_imag, out, work
):
    tile_rows = 8
    tiles = INNER // tile_rows
    low_half = lax.broadcasted_iota(jnp.int32, (tile_rows, 2 * HALF), 1) < HALF

    def place(slab, tile):
        strip, part = tile // 4, tile % 4
        if slab:
            return part * 16 + strip % 16, strip // 16 * tile_rows
        return strip, part * tile_rows

    def odd_factor(a):
        angle = -2.0 * math.pi * a / RADIX
        return (
            jnp.where(low_half, 1.0, math.cos(angle)).astype(jnp.float32),
            jnp.where(low_half, 0.0, math.sin(angle)).astype(jnp.float32),
        )

    factors = [odd_factor(a) for a in range(HALF_RADIX)]

    for tile in range(tiles):
        rows = slice(tile * tile_rows, (tile + 1) * tile_rows)
        imag_rows = slice(INNER + tile * tile_rows, INNER + (tile + 1) * tile_rows)
        values = []
        for a in range(HALF_RADIX):
            pair = []
            for half in range(2):
                chunk, row = place(slab_in, (half * HALF_RADIX + a) * tiles + tile)
                pair.append(chunks[chunk, row : row + tile_rows, :])
            total, rest = pair[0] + pair[1], pair[0] - pair[1]
            value = (
                jnp.where(low_half, total, swap_halves(rest)),
                jnp.where(low_half, swap_halves(total), rest),
            )
            values.append(scale(value, *factors[a]) if a else value)
        for k, value in enumerate(butterfly8(values, -1.0)):
            real, imag = scale(value, twiddle[0, k, rows], twiddle[1, k, rows])
            work[k, rows] = real
            work[k, imag_rows] = imag

    def multiply(matrix, value):
        high, low = split_value(value)
        return jnp.dot(
            matrix[...],
            jnp.concatenate([high, high, low], axis=0),
            preferred_element_type=jnp.float32,
        )

    for pair in range(0, HALF_RADIX, 2):
        value = multiply(left, jnp.concatenate([work[pair], work[pair + 1]], axis=1))
        factor = [
            jnp.concatenate([table[pair], table[pair + 1]], axis=1)
            for table in (prop_real, prop_imag)
        ]
        value = jnp.concatenate(scale((value[:INNER], value[INNER:]), *factor), axis=0)
        value = multiply(left_inverse, value)
        work[pair] = value[:, :INNER]
        work[pair + 1] = value[:, INNER:]

    for tile in range(tiles):
        rows = slice(tile * tile_rows, (tile + 1) * tile_rows)
        imag_rows = slice(INNER + tile * tile_rows, INNER + (tile + 1) * tile_rows)
        values = [
            scale((work[k, rows], work[k, imag_rows]), twiddle[0, k, rows], -twiddle[1, k, rows])
            for k in range(HALF_RADIX)
        ]
        for a, value in enumerate(butterfly8(values, 1.0)):
            if a:
                value = scale(value, factors[a][0], -factors[a][1])
            real, imag = value
            total = jnp.where(low_half, real, swap_halves(imag))
            rest = jnp.where(low_half, swap_halves(real), imag)
            for half, result in enumerate((total + rest, total - rest)):
                chunk, row = place(True, (half * HALF_RADIX + a) * tiles + tile)
                out[chunk, row : row + tile_rows, :] = result


def spectral_step(chunks, matrices, twiddle, propagators, slab_in):
    return pl.pallas_call(
        functools.partial(spectral_kernel, slab_in),
        out_shape=CHUNKS,
        in_specs=[whole()] * 6,
        out_specs=whole(),
        scratch_shapes=[pltpu.VMEM((HALF_RADIX, 2 * INNER, 2 * HALF), jnp.float32)],
        compiler_params=params(),
        name="spectral_step",
    )(chunks, *matrices, twiddle, *propagators)


def wavenumber(index):
    signed = jnp.where(index < SIZE // 2, index, index - SIZE).astype(jnp.float32)
    return signed * (2.0 * math.pi / (SIZE * grid_step))


def propagator_tables(angular, block):
    lane = jnp.arange(2 * HALF, dtype=jnp.int32)
    column = block // 2 + RADIX * ((block % 2) * HALF + lane % HALF)
    wave_y = wavenumber(column)[None, None, :]
    row = (
        jnp.arange(HALF_RADIX, dtype=jnp.int32)[:, None, None]
        + HALF_RADIX * jnp.arange(INNER, dtype=jnp.int32)[None, :, None]
    )
    wave_x = wavenumber(2 * row + lane // HALF)
    vertical_sq = angular * angular - wave_x * wave_x - wave_y * wave_y
    vertical = jnp.sqrt(jnp.abs(vertical_sq))
    propagating = vertical_sq > 0
    sine, cosine = sine_cosine(depth_step * vertical)
    real_part = jnp.where(propagating, cosine, jnp.exp(-depth_step * vertical))
    imag_part = jnp.where(propagating, sine, 0.0)
    return real_part, imag_part


def per_device(source_field, recorded, phase_index, slowness, slice_index):
    freq = lax.axis_index("zh")
    freqs = lax.axis_size("zh")
    angular = 0.5 + 1.5 * (freq.astype(jnp.float32) + 0.5) / freqs
    slab = ("xh", "c", "zl", "y", "xl")
    right = [jnp.asarray(t) for t in lane_tables()]
    left = [jnp.asarray(t) for t in row_tables()]
    lane_twiddle = jnp.asarray(lane_twiddles())
    row_twiddle = jnp.asarray(row_twiddles())
    propagators = propagator_tables(angular, lax.axis_index(slab) % (2 * RADIX))

    chunks, parts = first_step(
        phase_index, slice_index, source_field, recorded, right[0], lane_twiddle, slowness
    )
    up = [(z, (z + 1) % freqs) for z in range(freqs)]
    down = [(z, (z - 1) % freqs) for z in range(freqs)]
    middle = DEPTHS // 2
    below = lax.ppermute(parts, "zh", up)
    above = lax.ppermute(parts, "zh", down)
    chunks = lax.all_to_all(chunks, ("xh", "c"), 0, 0, tiled=True)
    chunks, below, above = lax.optimization_barrier((chunks, below, above))
    far = [
        lax.ppermute(below[:middle], "zh", up),
        lax.ppermute(above[middle:], "zh", down),
    ]
    chunks = lax.all_to_all(chunks, ("zh", "zl", "y", "xl"), 0, 0, tiled=True)
    chunks, far = lax.optimization_barrier((chunks, far))
    pictures = []
    for descent in range(DEPTHS):
        last = descent == DEPTHS - 1
        chunks = spectral_step(chunks, left, row_twiddle, propagators, descent > 0)
        chunks = lax.all_to_all(chunks, slab, 0, 0, tiled=True)
        late, at = divmod(descent, middle)
        slow = [(parts, descent), (below, descent), (far[late], at), (above, descent)]
        result = space_step(chunks, slow, right, lane_twiddle, last)
        pictures.append(result[-1])
        if not last:
            chunks = lax.all_to_all(result[0], slab, 0, 0, tiled=True)
    picture = jnp.stack(pictures, axis=2)
    picture = picture.reshape((freqs * freqs,) + picture.shape[2:])
    picture = lax.all_to_all(picture, ("zh", "xh", "c"), 0, 0, tiled=True)
    picture = jnp.sum(picture.reshape((freqs, freqs) + picture.shape[1:]), axis=0)
    return picture.transpose(1, 0, 2, 3).reshape(DEPTHS, ROWS // 2, SIZE // freqs)


def solution(mesh):
    fine = Mesh(mesh.devices.reshape(2, 2, 4, 2, 4, 2), ("xh", "c", "zh", "zl", "y", "xl"))
    freq, strip = ("xh", "c"), ("zh", "zl", "y", "xl")
    placed = (
        P(None, freq, None, strip, None),
        P(None, freq, None, strip, None),
        P(),
        P(None, strip, None),
        P(),
    )
    return jax.shard_map(
        per_device, mesh=fine, in_specs=placed, out_specs=P(None, strip, freq), check_vma=False
    )
```

```python
import functools
import math

import jax
import jax.numpy as jnp
import numpy as np
from jax import lax
from jax.experimental import pallas as pl
from jax.experimental.pallas import tpu as pltpu
from jax.sharding import Mesh
from jax.sharding import PartitionSpec as P

DEPTHS = 4
PHASES = 8
SIZE = 2048
RADIX = 16
HALF_RADIX = RADIX // 2
INNER = SIZE // RADIX
HALF = 64
ROWS = 64
VMEM_LIMIT = 12 * 1024 * 1024
FIRST_VMEM_LIMIT = 56 * 1024 * 1024

grid_step = 4.0
depth_step = 8.0


def split_table(table):
    high = table.astype(jnp.bfloat16)
    low = (table - high.astype(np.float64)).astype(jnp.bfloat16)
    return high, low


def inner_dft(direction):
    index = np.arange(INNER)
    angle = direction * 2.0 * np.pi * (np.outer(index, index) % INNER) / INNER
    return np.cos(angle), np.sin(angle)


def lane_tables():
    cosine, sine = inner_dft(-1.0)
    real_columns = np.concatenate([cosine, -sine], axis=0)
    imag_columns = np.concatenate([sine, cosine], axis=0)
    forward = np.concatenate(
        [
            part[:, half * HALF : (half + 1) * HALF]
            for half in range(2)
            for part in (real_columns, imag_columns)
        ],
        axis=1,
    )
    cosine, sine = inner_dft(1.0)
    real_rows = np.concatenate([cosine, sine], axis=1)
    imag_rows = np.concatenate([-sine, cosine], axis=1)
    inverse = (
        np.concatenate(
            [
                part[half * HALF : (half + 1) * HALF]
                for half in range(2)
                for part in (real_rows, imag_rows)
            ],
            axis=0,
        )
        / SIZE
    )
    out = []
    for table in (forward, inverse):
        high, low = split_table(table)
        out.append(np.concatenate([high, low, high], axis=0))
    return out


def row_tables():
    out = []
    for direction, scale in ((-1.0, 1.0), (1.0, 1.0 / SIZE)):
        cosine, sine = inner_dft(direction)
        table = np.concatenate(
            [np.concatenate([cosine, -sine], axis=1), np.concatenate([sine, cosine], axis=1)]
        )
        high, low = split_table(table * scale)
        out.append(np.concatenate([high, low, high], axis=1))
    return out


def lane_twiddles():
    angle = -2.0 * np.pi * np.outer(np.arange(RADIX), np.arange(INNER)) / SIZE
    factors = np.concatenate([np.cos(angle), np.sin(angle)], axis=1)
    return np.broadcast_to(factors[:, None], (RADIX, 8, 2 * INNER)).astype(np.float32)


def row_twiddles():
    odd = (np.arange(2 * HALF) >= HALF).astype(np.int64)
    order = 2 * np.arange(HALF_RADIX)[:, None, None] + odd
    angle = -2.0 * np.pi * (order * np.arange(INNER)[None, :, None]) / SIZE
    return np.stack([np.cos(angle), np.sin(angle)]).astype(np.float32)


def add(a, b):
    return (a[0] + b[0], a[1] + b[1])


def sub(a, b):
    return (a[0] - b[0], a[1] - b[1])


def turn(a, s):
    return (-a[1], a[0]) if s > 0 else (a[1], -a[0])


def scale(a, c, s):
    return (a[0] * c - a[1] * s, a[0] * s + a[1] * c)


def butterfly4(a, b, c, d, direction):
    even_sum, even_diff = add(a, c), sub(a, c)
    odd_sum, odd_diff = add(b, d), turn(sub(b, d), direction)
    return [
        add(even_sum, odd_sum),
        add(even_diff, odd_diff),
        sub(even_sum, odd_sum),
        sub(even_diff, odd_diff),
    ]


def butterfly8(values, direction):
    even = butterfly4(*values[0::2], direction)
    odd = butterfly4(*values[1::2], direction)
    root = math.sqrt(0.5)

    def eighth(a):
        if direction > 0:
            return ((a[0] - a[1]) * root, (a[0] + a[1]) * root)
        return ((a[0] + a[1]) * root, (a[1] - a[0]) * root)

    odd[1] = eighth(odd[1])
    odd[2] = turn(odd[2], direction)
    odd[3] = turn(eighth(odd[3]), direction)
    return [add(e, o) for e, o in zip(even, odd)] + [sub(e, o) for e, o in zip(even, odd)]


def butterfly16(values, direction):
    first = [butterfly4(*values[m::4], direction) for m in range(4)]
    result = [None] * 16
    for k in range(4):
        column = []
        for m in range(4):
            value = first[m][k]
            power = m * k
            if power == 4:
                value = turn(value, direction)
            elif power:
                angle = direction * 2.0 * math.pi * power / 16
                value = scale(value, math.cos(angle), math.sin(angle))
            column.append(value)
        for m, value in enumerate(butterfly4(*column, direction)):
            result[k + 4 * m] = value
    return result


def swap_halves(value):
    return pltpu.roll(value, HALF, 1)


def split_value(value):
    high = value.astype(jnp.bfloat16)
    low = (value - high.astype(jnp.float32)).astype(jnp.bfloat16)
    return high, low


def sine_cosine(angle):
    turns = jnp.round(angle * (2.0 / math.pi))
    rest = angle - turns * 1.5703125
    rest = rest - turns * 4.8375129699707031e-4
    rest = rest - turns * 7.5497899548918821e-8
    square = rest * rest
    sine = rest + rest * square * (
        -1.6666654611e-1 + square * (8.3321608736e-3 - square * 1.9515295891e-4)
    )
    cosine = (
        1.0
        - 0.5 * square
        + square
        * square
        * (4.166664568298827e-2 + square * (-1.388731625493765e-3 + square * 2.443315711809948e-5))
    )
    quarter = turns.astype(jnp.int32)
    odd = (quarter & 1) == 1
    sine_out = jnp.where(odd, cosine, sine)
    cosine_out = jnp.where(odd, sine, cosine)
    sine_out = jnp.where((quarter & 2) == 2, -sine_out, sine_out)
    cosine_out = jnp.where(((quarter + 1) & 2) == 2, -cosine_out, cosine_out)
    return sine_out, cosine_out


def lanes(a):
    return slice(a * INNER, (a + 1) * INNER)


def forward_rows(wave, work, table, twiddle, out):
    for tile in range(ROWS // 8):
        rows = slice(tile * 8, tile * 8 + 8)
        values = [(wave[0, rows, lanes(a)], wave[1, rows, lanes(a)]) for a in range(RADIX)]
        values = butterfly16(values, -1.0)
        for k, (real, imag) in enumerate(values):
            if k:
                cosine = twiddle[k, :, :INNER]
                sine = twiddle[k, :, INNER:]
                real, imag = real * cosine - imag * sine, real * sine + imag * cosine
            work[k, rows, :INNER] = real
            work[k, rows, INNER:] = imag

    for group in range(0, RADIX, 4):
        value = work[group : group + 4].reshape(4 * ROWS, 2 * INNER)
        high, low = split_value(value)
        result = jnp.dot(
            jnp.concatenate([high, high, low], axis=1),
            table[...],
            preferred_element_type=jnp.float32,
        )
        result = result.reshape(4, ROWS, 2 * INNER)
        for k in range(4):
            for kind in range(2):
                for half in range(2):
                    out[(kind * RADIX + group + k) * 2 + half] = result[
                        k,
                        kind * (ROWS // 2) : (kind + 1) * (ROWS // 2),
                        half * INNER : (half + 1) * INNER,
                    ]


def inverse_rows(chunks, work, table, twiddle, wave):
    for group in range(0, RADIX, 4):
        parts = []
        for k in range(4):
            for kind in range(2):
                place = (kind * RADIX + group + k) * 2
                parts.append(jnp.concatenate([chunks[place], chunks[place + 1]], axis=1))
        high, low = split_value(jnp.concatenate(parts, axis=0))
        result = jnp.dot(
            jnp.concatenate([high, high, low], axis=1),
            table[...],
            preferred_element_type=jnp.float32,
        )
        work[group : group + 4] = result.reshape(4, ROWS, 2 * INNER)

    for tile in range(ROWS // 8):
        rows = slice(tile * 8, tile * 8 + 8)
        values = []
        for k in range(RADIX):
            real, imag = work[k, rows, :INNER], work[k, rows, INNER:]
            if k:
                cosine = twiddle[k, :, :INNER]
                sine = twiddle[k, :, INNER:]
                real, imag = real * cosine + imag * sine, imag * cosine - real * sine
            values.append((real, imag))
        values = butterfly16(values, 1.0)
        for a, (real, imag) in enumerate(values):
            wave[0, rows, lanes(a)] = real
            wave[1, rows, lanes(a)] = imag


def rotate_and_image(wave, slow, places, freq, angular, image, keep):
    half_rows = ROWS // 2
    strips, part_rows = image.shape[0], image.shape[2]
    width = image.shape[3]

    for turn in range(strips):
        strip = lax.rem(freq + strips - turn, strips)
        first = pl.ds(pl.multiple_of(strip * part_rows, part_rows), part_rows)
        second = pl.ds(pl.multiple_of(half_rows + strip * part_rows, part_rows), part_rows)
        for a in range(SIZE // 512):
            columns = slice(a * 512, (a + 1) * 512)
            sine, cosine = sine_cosine(angular * (slow[turn][places[turn], :, columns] - 1.0))
            turned = []
            for rows in (first, second):
                real, imag = wave[0, rows, columns], wave[1, rows, columns]
                real, imag = real * cosine - imag * sine, real * sine + imag * cosine
                if keep:
                    wave[0, rows, columns] = real
                    wave[1, rows, columns] = imag
                turned.append((real, imag))
            picture = turned[0][0] * turned[1][0] - turned[0][1] * turned[1][1]
            place = a * 512 // width
            offset = a * 512 % width
            image[place, strip, :, offset : offset + 512] = picture * (1.0 / strips)


def fetch(pairs, semaphores):
    copies = [
        pltpu.make_async_copy(source, target, semaphores.at[n])
        for n, (source, target) in enumerate(pairs)
    ]
    for copy in copies:
        copy.start()
    return copies


def first_kernel(
    phases,
    places,
    turns,
    source,
    recorded,
    table,
    twiddle,
    slowness,
    out,
    parts,
    wave,
    work,
    fields,
    tables,
    factors,
    semaphores,
):
    half_rows = ROWS // 2
    group = lax.axis_index("xh") * lax.axis_size("c") + lax.axis_index("c")
    part_rows = parts.shape[1]
    part = pl.ds(pl.multiple_of(group * part_rows, part_rows), part_rows)
    copies = fetch(
        [
            (source, fields.at[0]),
            (recorded, fields.at[1]),
            (table, tables),
            (twiddle, factors),
        ]
        + [(slowness.at[places[d], part], parts.at[d]) for d in range(DEPTHS)],
        semaphores,
    )
    shots = fields.shape[1]
    levels = [phases[0, shot, group] & (PHASES - 1) for shot in range(shots)]
    angles = [(turns[0, level], turns[1, level]) for level in levels]
    for kind in range(2):
        copies[kind].wait()

        for tile in range(half_rows // 16):
            rows = slice(tile * 16, tile * 16 + 16)
            place = slice(kind * half_rows + tile * 16, kind * half_rows + tile * 16 + 16)
            for a in range(SIZE // 512):
                columns = slice(a * 512, (a + 1) * 512)
                real_sum, imag_sum = None, None
                for shot in range(shots):
                    real = fields[kind, shot, 0, 0, rows, columns].astype(jnp.float32)
                    imag = fields[kind, shot, 0, 1, rows, columns].astype(jnp.float32)
                    cosine, sine = angles[shot]
                    real_part = cosine * real - sine * imag
                    imag_part = cosine * imag + sine * real
                    real_sum = real_part if real_sum is None else real_sum + real_part
                    imag_sum = imag_part if imag_sum is None else imag_sum + imag_part
                wave[0, place, columns] = real_sum
                wave[1, place, columns] = imag_sum if kind == 0 else -imag_sum

    for copy in copies[2:4]:
        copy.wait()
    forward_rows(wave, work, tables, factors, out)
    for copy in copies[4:]:
        copy.wait()


def space_kernel(places, last, chunks, inverse_table, table, twiddle, *refs):
    strips = len(places)
    slow, refs = refs[:strips], refs[strips:]
    if last:
        image, wave, work = refs
    else:
        out, image, wave, work = refs
    freq = lax.axis_index("zh")
    angular = depth_step * (0.5 + 1.5 * (freq.astype(jnp.float32) + 0.5) / strips)
    inverse_rows(chunks, work, inverse_table, twiddle, wave)
    rotate_and_image(wave, slow, places, freq, angular, image, not last)
    if not last:
        forward_rows(wave, work, table, twiddle, out)


WAVE = pltpu.VMEM((2, ROWS, SIZE), jnp.float32)
WORK = pltpu.VMEM((RADIX, ROWS, 2 * INNER), jnp.float32)
CHUNKS = jax.ShapeDtypeStruct((64, ROWS // 2, 2 * HALF), jnp.float32)


def whole():
    return pl.BlockSpec(memory_space=pltpu.VMEM)


def anywhere():
    return pl.BlockSpec(memory_space=pl.ANY)


def scalars():
    return pl.BlockSpec(memory_space=pltpu.SMEM)


def params():
    return pltpu.CompilerParams(vmem_limit_bytes=VMEM_LIMIT)


def first_step(phases, places, source, recorded, table, twiddle, slowness):
    angle = np.arange(PHASES) * (2.0 * np.pi / PHASES)
    turns = jnp.asarray(np.stack([np.cos(angle), np.sin(angle)]).astype(np.float32))
    part_rows = ROWS // 2 // phases.shape[2]
    return pl.pallas_call(
        first_kernel,
        out_shape=[
            CHUNKS,
            jax.ShapeDtypeStruct((DEPTHS, part_rows, SIZE), jnp.float32),
        ],
        in_specs=[scalars()] * 3 + [anywhere()] * 5,
        out_specs=[whole(), whole()],
        scratch_shapes=[
            WAVE,
            WORK,
            pltpu.VMEM((2,) + source.shape, source.dtype),
            pltpu.VMEM(table.shape, table.dtype),
            pltpu.VMEM(twiddle.shape, twiddle.dtype),
            pltpu.SemaphoreType.DMA((4 + DEPTHS,)),
        ],
        compiler_params=pltpu.CompilerParams(vmem_limit_bytes=FIRST_VMEM_LIMIT),
        name="encode_forward",
    )(phases, places, turns, source, recorded, table, twiddle, slowness)


def space_step(chunks, slow, tables, twiddle, last):
    slow, places = zip(*slow)
    parts = len(slow)
    part = slow[0].shape[1:]
    image = jax.ShapeDtypeStruct((parts, parts, part[0], SIZE // parts), jnp.float32)
    out_shape = [image] if last else [CHUNKS, image]
    return pl.pallas_call(
        functools.partial(space_kernel, places, last),
        out_shape=out_shape,
        in_specs=[whole()] * (4 + parts),
        out_specs=[whole()] * len(out_shape),
        scratch_shapes=[
            WAVE,
            WORK,
        ],
        compiler_params=params(),
        name="space_last" if last else "space_step",
    )(chunks, tables[1], tables[0], twiddle, *slow)


def spectral_kernel(
    slab_in, chunks, left, left_inverse, twiddle, prop_real, prop_imag, out, work
):
    tile_rows = 8
    tiles = INNER // tile_rows
    low_half = lax.broadcasted_iota(jnp.int32, (tile_rows, 2 * HALF), 1) < HALF

    def place(slab, tile):
        strip, part = tile // 4, tile % 4
        if slab:
            return part * 16 + strip % 16, strip // 16 * tile_rows
        return strip, part * tile_rows

    def odd_factor(a):
        angle = -2.0 * math.pi * a / RADIX
        return (
            jnp.where(low_half, 1.0, math.cos(angle)).astype(jnp.float32),
            jnp.where(low_half, 0.0, math.sin(angle)).astype(jnp.float32),
        )

    factors = [odd_factor(a) for a in range(HALF_RADIX)]

    for tile in range(tiles):
        rows = slice(tile * tile_rows, (tile + 1) * tile_rows)
        imag_rows = slice(INNER + tile * tile_rows, INNER + (tile + 1) * tile_rows)
        values = []
        for a in range(HALF_RADIX):
            pair = []
            for half in range(2):
                chunk, row = place(slab_in, (half * HALF_RADIX + a) * tiles + tile)
                pair.append(chunks[chunk, row : row + tile_rows, :])
            total, rest = pair[0] + pair[1], pair[0] - pair[1]
            value = (
                jnp.where(low_half, total, swap_halves(rest)),
                jnp.where(low_half, swap_halves(total), rest),
            )
            values.append(scale(value, *factors[a]) if a else value)
        for k, value in enumerate(butterfly8(values, -1.0)):
            real, imag = scale(value, twiddle[0, k, rows], twiddle[1, k, rows])
            work[k, rows] = real
            work[k, imag_rows] = imag

    def multiply(matrix, value):
        high, low = split_value(value)
        return jnp.dot(
            matrix[...],
            jnp.concatenate([high, high, low], axis=0),
            preferred_element_type=jnp.float32,
        )

    for pair in range(0, HALF_RADIX, 2):
        value = multiply(left, jnp.concatenate([work[pair], work[pair + 1]], axis=1))
        factor = [
            jnp.concatenate([table[pair], table[pair + 1]], axis=1)
            for table in (prop_real, prop_imag)
        ]
        value = jnp.concatenate(scale((value[:INNER], value[INNER:]), *factor), axis=0)
        value = multiply(left_inverse, value)
        work[pair] = value[:, :INNER]
        work[pair + 1] = value[:, INNER:]

    for tile in range(tiles):
        rows = slice(tile * tile_rows, (tile + 1) * tile_rows)
        imag_rows = slice(INNER + tile * tile_rows, INNER + (tile + 1) * tile_rows)
        values = [
            scale((work[k, rows], work[k, imag_rows]), twiddle[0, k, rows], -twiddle[1, k, rows])
            for k in range(HALF_RADIX)
        ]
        for a, value in enumerate(butterfly8(values, 1.0)):
            if a:
                value = scale(value, factors[a][0], -factors[a][1])
            real, imag = value
            total = jnp.where(low_half, real, swap_halves(imag))
            rest = jnp.where(low_half, swap_halves(real), imag)
            for half, result in enumerate((total + rest, total - rest)):
                chunk, row = place(True, (half * HALF_RADIX + a) * tiles + tile)
                out[chunk, row : row + tile_rows, :] = result


def spectral_step(chunks, matrices, twiddle, propagators, slab_in):
    return pl.pallas_call(
        functools.partial(spectral_kernel, slab_in),
        out_shape=CHUNKS,
        in_specs=[whole()] * 6,
        out_specs=whole(),
        scratch_shapes=[pltpu.VMEM((HALF_RADIX, 2 * INNER, 2 * HALF), jnp.float32)],
        compiler_params=params(),
        name="spectral_step",
    )(chunks, *matrices, twiddle, *propagators)


def wavenumber(index):
    signed = jnp.where(index < SIZE // 2, index, index - SIZE).astype(jnp.float32)
    return signed * (2.0 * math.pi / (SIZE * grid_step))


def propagator_tables(angular, block):
    lane = jnp.arange(2 * HALF, dtype=jnp.int32)
    column = block // 2 + RADIX * ((block % 2) * HALF + lane % HALF)
    wave_y = wavenumber(column)[None, None, :]
    row = (
        jnp.arange(HALF_RADIX, dtype=jnp.int32)[:, None, None]
        + HALF_RADIX * jnp.arange(INNER, dtype=jnp.int32)[None, :, None]
    )
    wave_x = wavenumber(2 * row + lane // HALF)
    vertical_sq = angular * angular - wave_x * wave_x - wave_y * wave_y
    vertical = jnp.sqrt(jnp.abs(vertical_sq))
    propagating = vertical_sq > 0
    sine, cosine = sine_cosine(depth_step * vertical)
    real_part = jnp.where(propagating, cosine, jnp.exp(-depth_step * vertical))
    imag_part = jnp.where(propagating, sine, 0.0)
    return real_part, imag_part


def per_device(source_field, recorded, phase_index, slowness, slice_index):
    freq = lax.axis_index("zh")
    freqs = lax.axis_size("zh")
    angular = 0.5 + 1.5 * (freq.astype(jnp.float32) + 0.5) / freqs
    slab = ("xh", "c", "zl", "y", "xl")
    right = [jnp.asarray(t) for t in lane_tables()]
    left = [jnp.asarray(t) for t in row_tables()]
    lane_twiddle = jnp.asarray(lane_twiddles())
    row_twiddle = jnp.asarray(row_twiddles())
    propagators = propagator_tables(angular, lax.axis_index(slab) % (2 * RADIX))

    chunks, parts = first_step(
        phase_index, slice_index, source_field, recorded, right[0], lane_twiddle, slowness
    )
    up = [(z, (z + 1) % freqs) for z in range(freqs)]
    down = [(z, (z - 1) % freqs) for z in range(freqs)]
    middle = DEPTHS // 2
    below = lax.ppermute(parts, "zh", up)
    above = lax.ppermute(parts, "zh", down)
    chunks = lax.all_to_all(chunks, ("xh", "c"), 0, 0, tiled=True)
    chunks, below, above = lax.optimization_barrier((chunks, below, above))
    far = [
        lax.ppermute(below[:middle], "zh", up),
        lax.ppermute(above[middle:], "zh", down),
    ]
    chunks = lax.all_to_all(chunks, ("zh", "zl", "y", "xl"), 0, 0, tiled=True)
    chunks, far = lax.optimization_barrier((chunks, far))
    pictures = []
    for descent in range(DEPTHS):
        last = descent == DEPTHS - 1
        chunks = spectral_step(chunks, left, row_twiddle, propagators, descent > 0)
        chunks = lax.all_to_all(chunks, slab, 0, 0, tiled=True)
        late, at = divmod(descent, middle)
        slow = [(parts, descent), (below, descent), (far[late], at), (above, descent)]
        result = space_step(chunks, slow, right, lane_twiddle, last)
        pictures.append(result[-1])
        if not last:
            chunks = lax.all_to_all(result[0], slab, 0, 0, tiled=True)
    picture = jnp.stack(pictures, axis=2)
    picture = picture.reshape((freqs * freqs,) + picture.shape[2:])
    picture = lax.all_to_all(picture, ("xh", "c", "zh"), 0, 0, tiled=True)
    picture = jnp.sum(picture.reshape((freqs, freqs) + picture.shape[1:]), axis=1)
    return picture.transpose(1, 0, 2, 3).reshape(DEPTHS, ROWS // 2, SIZE // freqs)


def solution(mesh):
    fine = Mesh(mesh.devices.reshape(2, 2, 4, 2, 4, 2), ("xh", "c", "zh", "zl", "y", "xl"))
    freq, strip = ("xh", "c"), ("zh", "zl", "y", "xl")
    placed = (
        P(None, freq, None, strip, None),
        P(None, freq, None, strip, None),
        P(),
        P(None, strip, None),
        P(),
    )
    return jax.shard_map(
        per_device, mesh=fine, in_specs=placed, out_specs=P(None, strip, freq), check_vma=False
    )
```
